32 devices in a mesh: tm: 8 (over z, core), expert: 4 (over y, x).
Axes of the slice: x: 2, y: 2, z: 4, core: 2. Of those that a mesh axis runs over, the one named last changes fastest.
Arguments:
- frames: bfloat16 [2, 2048, 1536], P(None, ('tm', 'expert')), may hold values from -6 to 6
- expert_out: bfloat16 [2, 8, 4, 32, 8, 1536], P(None, 'tm', None, 'expert'), may hold values from -6 to 6
- routes: int32 [2, 2048, 2], P(None, ('tm', 'expert')), may hold values from 0 to 31, all different within a row; in each aligned block of 64 rows (0 to 63, 64 to 127, ..., all dimensions but the last counted through in order) at most 8 rows name the same one
- order: int32 [2, 32, 64], P(None, ('tm', 'expert')), may hold values from 0 to 63, each once within a row
- probs: float32 [2, 2048, 2], P(None, ('tm', 'expert')), may hold values from 0.05 to 1
- lengths: int32 [2, 8], replicated, may hold values from 1 to 1024, 2048 in all within a row
- gain: float32 [1536], replicated, may hold values from 0.1 to 1.9
- kernel: float32 [31, 1536], replicated, may hold values from -1 to 1
- grad_out: bfloat16 [2, 2048, 1536], P(None, ('tm', 'expert')), may hold values from -6 to 6
Outputs:
- grad_x: bfloat16 [2, 2048, 1536], P(None, ('tm', 'expert'))
- grad_expert: bfloat16 [2, 8, 4, 32, 8, 1536], P(None, 'tm', None, 'expert')
- grad_probs: float32 [2, 2048, 2], P(None, ('tm', 'expert'))
- grad_kernel: float32 [31, 1536], P(None, 'expert')
- grad_gain: float32 [1536], P('expert')
The draws below stay inside these ranges and needn't reach their ends.
Inputs may be any that keep to these rules, and one draw needn't show every extreme that they name: `routes`: the two experts of a frame differ; among the 64 frames of one time block of one micro-batch no expert is named more than 8 times, a bound that some block reaches. `order`: each time block's row holds every number of 0 .. 63 once. Each micro-batch's lengths sum to 2048; the largest is exactly 1024.
All inputs are finite; a program needn't handle non-finite values.
Results may differ from the reference program's by a relative error of at most 0.0056.
Values may be sent and summed in bfloat16 or wider, within the bound.
No kernel may reach another device: no remote copies, remote signals or barrier semaphores. Data moves between devices by JAX's collectives and lax.ppermute only.
A program may use at most 64 MiB of HBM per device.

```python
import math
import jax
import jax.numpy as jnp
import numpy as np
from jax import lax

D = 1536
EXPERTS = 32
KW = 31
MICRO = 2
F_DEV = 64
HALF = 15
CAP = 8
GROUPS = 8
SOURCES = 4
BLOCKS = 32
FRAMES = 2048
UTTS = 8
MAXLEN = 1024


def with_spikes(entries, key, source, target, blocks, factor):
    def block_of(position):
        return (jnp.arange(entries.shape[position]) // (entries.shape[position] // blocks)).reshape((-1,) + (1,) * (entries.ndim - 1 - position))

    near = jax.random.permutation(key, blocks)[block_of(target)]
    far = (block_of(target) + blocks // 2) % blocks
    return jnp.where((block_of(source) == near) | (block_of(source) == far), factor * entries, entries)


def shard_levels(own_key, dims, shards, low, high):
    def one(position, parts):
        heights = jax.random.uniform(jax.random.fold_in(jax.random.fold_in(own_key, 6), position), (parts,), jnp.float32, low / len(shards), high / len(shards))
        return jnp.repeat(jnp.exp(heights), dims[position] // parts).reshape((-1,) + (1,) * (len(dims) - position - 1))

    level = one(*shards[0])
    for cut in shards[1:]:
        level = level * one(*cut)
    return level


def length_profile(count, total, most, lean):
    portions = [(1 << 20) // math.isqrt(grade ** lean) + 1 for grade in range(2, count + 1)]
    rest, holding = total - most - (count - 1), [1] * (count - 1)
    while rest > 0:
        free = [i for i in range(count - 1) if holding[i] < most]
        whole, left = sum([portions[i] for i in free]), rest
        for i in free:
            extra = min(most - holding[i], max(1, left * portions[i] // whole), rest)
            holding[i] = holding[i] + extra
            rest = rest - extra
    return np.array([most] + holding)


def ragged(own_key, number_of, total, bound, lean):
    if number_of == 2:
        one = jax.random.randint(own_key, (), max(1, total - bound), min(bound, total - 1) + 1)
        return jnp.stack([one, total - one])
    sizes = jnp.asarray(length_profile(number_of, total, bound, lean), jnp.int32)
    twos = (number_of - 1) // 2
    donor, taker = sizes[1:1 + 2 * twos:2], sizes[2:2 + 2 * twos:2]
    room = jnp.minimum(donor - 1, bound - taker)
    shifted = jax.random.randint(jax.random.fold_in(own_key, 1), (twos,), 0, 1 << 20) % (room + 1)
    sizes = sizes.at[1:1 + 2 * twos:2].set(donor - shifted).at[2:2 + 2 * twos:2].set(taker + shifted)
    return sizes[jax.random.permutation(jax.random.fold_in(own_key, 2), number_of)]


def shared_out(key, own, number, rows, amount, top, limit, skew):
    ranking = jax.random.permutation(key, amount)
    packed, ordinary = shares(amount, rows * top, limit, skew, True), shares(amount, rows * top, limit, skew, False)
    places = jnp.arange(amount)

    def named(sizes, turn):
        used = int((sizes > 0).sum())
        fixed = max(1, used // 4)
        shifted = fixed + (places - fixed + turn * (used - fixed)) % max(1, amount - fixed)
        return jnp.zeros((amount,), jnp.int32).at[ranking[jnp.where(places < fixed, places, shifted)]].set(jnp.asarray(sizes, jnp.int32))

    sizes = jnp.where(number % 4 == 0, named(packed, number // 4), named(ordinary, number - number // 4 - 1))
    mixed = jax.random.permutation(jax.random.fold_in(own, 3), amount)
    giver, sink = mixed[0:amount // 2 * 2:2], mixed[1:amount // 2 * 2:2]
    slack = jnp.minimum(sizes[giver] - 1, limit - sizes[sink]) // 2
    slack = jnp.where((giver == ranking[0]) | (sink == ranking[0]) | (sizes[sink] == 0), 0, jnp.maximum(slack, 0))
    shifted = jax.random.randint(jax.random.fold_in(own, 4), (amount // 2,), 0, 1 << 20) % (slack + 1)
    sizes = sizes.at[giver].add(-shifted).at[sink].add(shifted)
    members = jnp.searchsorted(jnp.cumsum(sizes), jnp.arange(rows * top), side="right").astype(jnp.int32)
    grid = members.reshape(top, rows).T
    grid = grid[jax.random.permutation(jax.random.fold_in(own, 1), rows)]
    turn = jax.random.randint(jax.random.fold_in(own, 2), (rows, 1), 0, top)
    return jnp.take_along_axis(grid, (jnp.arange(top)[None, :] + turn) % top, axis=1)


def shares(number_of, total, most, skew, full):
    weights = [(1 << 20) // math.isqrt(grade ** skew) + 1 for grade in range(1, number_of + 1)]
    largest = most if full else min(most, max(-(-total // number_of), total * weights[0] // sum(weights)))
    least = 1 if total - largest >= number_of - 1 else 0
    given, surplus = [largest] + [least] * (number_of - 1), total - largest - least * (number_of - 1)
    while surplus > 0:
        movable = [i for i in range(1, number_of) if given[i] < largest] or [i for i in range(1, number_of) if given[i] < most]
        whole, remaining = sum([weights[i] for i in movable]), surplus
        for i in movable:
            more = min(most - given[i], max(1, remaining * weights[i] // whole), surplus)
            given[i] = given[i] + more
            surplus = surplus - more
    return np.array(given)


def gaussian(own_key, extent, deviation, bound, shards=(), held_as=jnp.bfloat16):
    values = deviation * jax.random.normal(own_key, extent, jnp.float32)
    if shards:
        values = values * shard_levels(own_key, extent, shards, -0.22, 0.18)
    return jnp.clip(values, -bound, bound).astype(held_as)


def bell_draw_with(stream_key, shape, spread, bound, cuts, heavy, kind=jnp.bfloat16):
    drawn = spread * jax.random.normal(stream_key, shape, jnp.float32)
    if cuts:
        drawn = drawn * shard_levels(stream_key, shape, cuts, -0.22, 0.18)
    return jnp.clip(with_spikes(drawn, jax.random.fold_in(stream_key, 3), *heavy), -bound, bound).astype(kind)


def setup_inputs(seed: int = 0) -> dict:
    splits = jax.random.split(jax.random.key(seed), 10)
    frames = gaussian(splits[0], (MICRO, FRAMES, D), 1.0, 6.0, ((1, 32),))
    expert_out = gaussian(splits[1], (MICRO, GROUPS, SOURCES, EXPERTS, CAP, D), 1.0, 6.0, ((1, 8), (3, 4)))
    routes_keys = jax.random.split(jax.random.fold_in(splits[2], 1), MICRO * FRAMES // F_DEV)
    routes_turns = jax.random.permutation(jax.random.fold_in(splits[2], 3), MICRO * FRAMES // F_DEV)
    routes = jax.vmap(lambda own, number: shared_out(jax.random.fold_in(splits[2], 2), own, number, F_DEV, EXPERTS, 2, CAP, 2))(routes_keys, routes_turns).reshape((MICRO, FRAMES, 2))
    order = jax.vmap(lambda own: jax.random.permutation(own, F_DEV))(jax.random.split(splits[3], MICRO * BLOCKS)).reshape((MICRO, BLOCKS, F_DEV)).astype(jnp.int32)
    probs = jnp.clip(0.05 + 0.95 * jax.random.uniform(splits[4], (MICRO, FRAMES, 2), jnp.float32) ** shard_levels(splits[4], (MICRO, FRAMES, 2), ((1, 32),), -0.2, 0.2), 0.05, 1.0)
    lengths = jax.vmap(lambda own: ragged(own, UTTS, FRAMES, MAXLEN, 1))(jax.random.split(splits[5], MICRO)).reshape((MICRO, UTTS)).astype(jnp.int32)
    gain = jnp.clip(1.0 + 0.18 * jax.random.normal(splits[6], (D,), jnp.float32), 0.1, 1.9)
    kernel = gaussian(splits[7], (KW, D), KW ** -0.5, 1.0, (), jnp.float32)
    grad_out = bell_draw_with(splits[8], (MICRO, FRAMES, D), 1.0, 6.0, ((1, 32),), (1, 2, 32, 2.75))
    return dict(frames=frames, expert_out=expert_out, routes=routes, order=order, probs=probs, lengths=lengths, gain=gain, kernel=kernel, grad_out=grad_out)


def slot_table(route_rows, order_row):
    row_count = route_rows.shape[0]
    sort_keys = (order_row.astype(jnp.int32)[:, None] * 2 + jnp.arange(2, dtype=jnp.int32)[None, :]).reshape(-1)
    owners = route_rows.astype(jnp.int32).reshape(-1)
    before = (owners[:, None] == owners[None, :]) & (sort_keys[None, :] < sort_keys[:, None])
    return lax.optimization_barrier(jnp.sum(before.astype(jnp.int32), axis=1)).astype(jnp.int32).reshape(row_count, 2)

def utterance_of(positions, lengths_row):
    utt_ends = jnp.cumsum(lengths_row.astype(jnp.int32)).astype(jnp.int32)
    return lax.optimization_barrier(jnp.sum((positions[:, None] >= utt_ends[None, :]).astype(jnp.int32), axis=1)).astype(jnp.int32)

def neighbour_masks(seg_padded, row_count):
    centre = seg_padded[HALF:HALF + row_count]
    return [(seg_padded[offset:offset + row_count] == centre).astype(jnp.float32)[:, None] for offset in range(KW)]

def conv_forward(padded, kernel_part, masks, row_count):
    running = jnp.zeros((row_count, padded.shape[1]), jnp.float32)
    for offset in range(KW):
        running = running + kernel_part[offset][None, :] * (padded[offset:offset + row_count].astype(jnp.float32) * masks[offset])
    return running

def swish_slope(values):
    sigmoid_v = jax.nn.sigmoid(values)
    return sigmoid_v * (1.0 + values * (1.0 - sigmoid_v))

def conv_backward(padded, grad_padded, grad_mid, kernel_part, masks, row_count):
    running = jnp.zeros((row_count, padded.shape[1]), jnp.float32)
    grad_float = grad_mid.astype(jnp.float32)
    kernel_rows = []
    for offset in range(KW):
        running = running + kernel_part[KW - 1 - offset][None, :] * (grad_padded[offset:offset + row_count].astype(jnp.float32) * masks[offset])
        kernel_rows.append(lax.optimization_barrier(jnp.sum(padded[offset:offset + row_count].astype(jnp.float32) * masks[offset] * grad_float, axis=0)))
    return (running.astype(jnp.bfloat16), jnp.stack(kernel_rows))

def pick_rows(buffer_rows, slot_index):
    return buffer_rows[slot_index]

def place_rows(buffer_rows, slot_index, values):
    return buffer_rows.at[slot_index].set(values)

def reference(frames, expert_out, routes, order, probs, lengths, gain, kernel, grad_out):
    scale_norm = 1.0 / math.sqrt(MICRO * FRAMES)
    kernel_sum = jnp.zeros((KW, D), jnp.float32)
    gain_sum = jnp.zeros((D,), jnp.float32)
    grad_x_list = []
    grad_expert_list = []
    grad_probs_list = []
    for micro in range(MICRO):
        route_blocks = routes[micro].astype(jnp.int32).reshape(BLOCKS, F_DEV, 2)
        slot_blocks = jax.vmap(slot_table)(route_blocks, order[micro])
        flat_index = (route_blocks * CAP + slot_blocks).reshape(BLOCKS, 2 * F_DEV).astype(jnp.int32)
        tables = expert_out[micro].reshape(BLOCKS, EXPERTS * CAP, D)
        picked = jax.vmap(pick_rows)(tables, flat_index).reshape(FRAMES, 2, D)
        weights = probs[micro]
        mixed = frames[micro].astype(jnp.float32) + weights[:, 0:1] * picked[:, 0].astype(jnp.float32) + weights[:, 1:2] * picked[:, 1].astype(jnp.float32)
        centre_mean = lax.optimization_barrier(jnp.mean(mixed, axis=1, keepdims=True))
        centred = mixed - centre_mean
        rstd = lax.rsqrt(lax.optimization_barrier(jnp.mean(centred * centred, axis=1, keepdims=True)) + 1e-05)
        nhat = centred * rstd
        conv_in = (nhat * gain[None, :]).astype(jnp.bfloat16)
        positions = jnp.arange(-HALF, FRAMES + HALF, dtype=jnp.int32)
        inside = (positions >= 0) & (positions < FRAMES)
        seg_padded = jnp.where(inside, utterance_of(positions, lengths[micro]), -1).astype(jnp.int32)
        masks = neighbour_masks(seg_padded, FRAMES)
        padded = jnp.pad(conv_in, ((HALF, HALF), (0, 0)))
        conv_out = conv_forward(padded, kernel, masks, FRAMES)
        grad_conv = (grad_out[micro].astype(jnp.float32) * swish_slope(conv_out)).astype(jnp.bfloat16)
        grad_padded = jnp.pad(grad_conv, ((HALF, HALF), (0, 0)))
        grad_in, kernel_terms = conv_backward(padded, grad_padded, grad_conv, kernel, masks, FRAMES)
        kernel_sum = kernel_sum + kernel_terms
        grad_in_f = grad_in.astype(jnp.float32)
        gain_sum = gain_sum + lax.optimization_barrier(jnp.sum(grad_in_f * nhat, axis=0))
        d_norm = grad_in_f * gain[None, :]
        dmixed = grad_out[micro].astype(jnp.float32) + rstd * (d_norm - lax.optimization_barrier(jnp.mean(d_norm, axis=1, keepdims=True)) - nhat * lax.optimization_barrier(jnp.mean(d_norm * nhat, axis=1, keepdims=True)))
        grad_x_list.append(dmixed.astype(jnp.bfloat16))
        grad_probs_list.append(lax.optimization_barrier(jnp.sum(dmixed[:, None, :] * picked.astype(jnp.float32), axis=2)))
        values = (weights[:, :, None] * dmixed[:, None, :]).astype(jnp.bfloat16).reshape(BLOCKS, 2 * F_DEV, D)
        empty = jnp.zeros((BLOCKS, EXPERTS * CAP, D), jnp.bfloat16)
        filled = jax.vmap(place_rows)(empty, flat_index, values)
        grad_expert_list.append(filled.reshape(GROUPS, SOURCES, EXPERTS, CAP, D))
    return (jnp.stack(grad_x_list), jnp.stack(grad_expert_list), jnp.stack(grad_probs_list), kernel_sum * scale_norm, gain_sum * scale_norm)
```

```python
import functools
import math

import jax
import jax.numpy as jnp
from jax import lax
from jax.experimental import pallas as pl
from jax.experimental.pallas import tpu as pltpu
from jax.sharding import PartitionSpec as P

EXPERTS = 32
KW = 31
HALF = 15
CAP = 8
SIDE = 32
GSIDE = 16
CHUNK = 256
F32 = jnp.float32
BF16 = jnp.bfloat16
VMEM_LIMIT = 48 * 1024 * 1024


def slot_table(route_rows, order_row):
    row_count = route_rows.shape[0]
    sort_keys = (order_row[:, None] * 2 + jnp.arange(2, dtype=jnp.int32)[None, :]).reshape(-1)
    owners = route_rows.reshape(-1)
    before = (owners[:, None] == owners[None, :]) & (sort_keys[None, :] < sort_keys[:, None])
    return jnp.sum(before.astype(jnp.int32), axis=1).reshape(row_count, 2)


def combine_kernel(
    group_count,
    place_ref,
    own_ref,
    *rest,
):
    table_refs = rest[: group_count - 1]
    frames_ref, flat_ref, probs_ref, gain_ref = rest[group_count - 1 : group_count + 3]
    conv_in_ref, send_ref, nhat_ref, rstd_ref, picked_ref = rest[group_count + 3 :]
    rows = frames_ref.shape[1]
    block = own_ref.shape[1] * own_ref.shape[2]
    width = frames_ref.shape[2]
    flat = flat_ref[0]
    probs = probs_ref[0]
    tables = [own_ref[...].reshape(block, width)] + [r[0] for r in table_refs]
    table = jnp.concatenate(tables, axis=0) if group_count > 1 else tables[0]
    lane = lax.broadcasted_iota(jnp.int32, (rows, group_count * block), 1)
    mixed = frames_ref[0].astype(F32)
    for k in range(2):
        hot = jnp.where(lane == flat[:, k : k + 1], 1.0, 0.0).astype(BF16)
        row = jnp.dot(hot, table, preferred_element_type=F32)
        picked_ref[k] = row.astype(BF16)
        mixed = mixed + probs[:, k : k + 1] * row
    mean = jnp.mean(mixed, axis=1, keepdims=True)
    centred = mixed - mean
    rstd = lax.rsqrt(jnp.mean(centred * centred, axis=1, keepdims=True) + 1e-05)
    nhat = centred * rstd
    nhat_ref[...] = nhat
    rstd_ref[...] = jnp.broadcast_to(rstd, rstd_ref.shape)
    conv_in = (nhat * gain_ref[...]).astype(BF16)
    conv_in_ref[...] = conv_in
    odd = place_ref[1]

    @pl.when(odd == 0)
    def _():
        send_ref[0] = conv_in[rows - SIDE :]
        send_ref[1] = conv_in[:SIDE]

    @pl.when(odd == 1)
    def _():
        send_ref[0] = conv_in[:SIDE]
        send_ref[1] = conv_in[rows - SIDE :]


def swish_slope(values):
    sigmoid_v = jax.nn.sigmoid(values)
    return sigmoid_v * (1.0 + values * (1.0 - sigmoid_v))


def conv_kernel(
    group_count,
    first,
    micro,
    frame_total,
    place_ref,
    lengths_ref,
    conv_in_ref,
    near_ref,
    far_ref,
    grad_out_ref,
    gnear_ref,
    gfar_ref,
    nhat_ref,
    rstd_ref,
    picked_ref,
    flat_row_ref,
    probs_ref,
    gain_ref,
    kernel_ref,
    *rest,
):
    if first:
        grad_x_ref, grad_probs_ref, terms_ref = rest[:3]
        rest = rest[3:]
        last_terms = None
    else:
        last_terms, _, _, grad_x_ref, grad_probs_ref, terms_ref = rest[:6]
        rest = rest[6:]
    out_refs = rest[:group_count]
    window, gout, shifts, gwin, gin, kacc = rest[group_count:]
    rows, width = conv_in_ref.shape
    mid = rows + 2 * GSIDE
    full = rows + 2 * SIDE
    odd = place_ref[1]
    chunks = width // CHUNK

    window[SIDE : SIDE + rows, :] = conv_in_ref[...]
    gout[GSIDE : GSIDE + rows, :] = grad_out_ref[0]

    @pl.when(odd == 0)
    def _():
        window[:SIDE, :] = far_ref[...]
        window[SIDE + rows :, :] = near_ref[...]
        gout[:GSIDE, :] = gfar_ref[0]
        gout[GSIDE + rows :, :] = gnear_ref[0]

    @pl.when(odd == 1)
    def _():
        window[:SIDE, :] = near_ref[...]
        window[SIDE + rows :, :] = far_ref[...]
        gout[:GSIDE, :] = gnear_ref[0]
        gout[GSIDE + rows :, :] = gfar_ref[0]

    gwin[: SIDE - GSIDE, :] = jnp.zeros((SIDE - GSIDE, CHUNK), BF16)
    gwin[SIDE - GSIDE + mid :, :] = jnp.zeros((SIDE - GSIDE, CHUNK), BF16)

    first_frame = place_ref[0]
    t_local = lax.broadcasted_iota(jnp.int32, (mid, full), 0)
    r_local = lax.broadcasted_iota(jnp.int32, (mid, full), 1)
    t_pos = first_frame - GSIDE + t_local
    r_pos = first_frame - SIDE + r_local

    def count(u, carry):
        end, t_seg, r_seg = carry
        end = end + lengths_ref[micro, u]
        return (
            end,
            t_seg + jnp.where(t_pos >= end, 1, 0),
            r_seg + jnp.where(r_pos >= end, 1, 0),
        )

    zero = jnp.zeros((mid, full), jnp.int32)
    _, t_seg, r_seg = lax.fori_loop(0, lengths_ref.shape[1], count, (0, zero, zero))
    same = (t_seg == r_seg) & (t_pos >= 0) & (t_pos < frame_total) & (r_pos >= 0) & (r_pos < frame_total)
    gap = jnp.where(same, r_local - t_local - (SIDE - GSIDE - HALF), -1)
    for i in range(KW):
        shifts[i * mid : (i + 1) * mid, :] = jnp.where(gap == i, 1.0, 0.0).astype(BF16)

    def chunk_step(q, carry):
        s1, s2 = carry
        cols = pl.ds(pl.multiple_of(q * CHUNK, CHUNK), CHUNK)
        taps = kernel_ref[:, cols]
        xw = window[:, cols]
        acc = jnp.zeros((mid, CHUNK), F32)
        for i in range(KW):
            v = jnp.dot(shifts[i * mid : (i + 1) * mid, :], xw, preferred_element_type=F32)
            acc = acc + taps[i : i + 1, :] * v
        g = (gout[:, cols].astype(F32) * swish_slope(acc)).astype(BF16)
        gwin[SIDE - GSIDE : SIDE - GSIDE + mid, :] = g
        gw = gwin[...]
        x = conv_in_ref[:, cols].astype(F32)
        acc = jnp.zeros((rows, CHUNK), F32)
        for j in range(KW):
            base = j * mid + GSIDE
            v = jnp.dot(shifts[base : base + rows, :], gw, preferred_element_type=F32)
            i = KW - 1 - j
            acc = acc + taps[i : i + 1, :] * v
            kacc[i : i + 1, cols] = jnp.sum(x * v, axis=0, keepdims=True)
        grad_in = acc.astype(BF16).astype(F32)
        nhat = nhat_ref[:, cols]
        kacc[KW : KW + 1, cols] = jnp.sum(grad_in * nhat, axis=0, keepdims=True)
        dn = grad_in * gain_ref[:, cols]
        gin[:, cols] = dn
        return (
            s1 + jnp.sum(dn, axis=1, keepdims=True),
            s2 + jnp.sum(dn * nhat, axis=1, keepdims=True),
        )

    none = jnp.zeros((rows, 1), F32)
    s1, s2 = lax.fori_loop(0, chunks, chunk_step, (none, none))
    m1 = s1 * (1.0 / width)
    m2 = s2 * (1.0 / width)
    rstd = rstd_ref[:, :1]
    probs = probs_ref[0]
    slots = out_refs[0].shape[0]
    total = slots * group_count
    spots = lax.broadcasted_iota(jnp.int32, (total, 2 * rows), 0)
    hot = jnp.where(spots == flat_row_ref[0], 1.0, 0.0).astype(BF16)

    def back_step(q, carry):
        p0, p1 = carry
        cols = pl.ds(pl.multiple_of(q * CHUNK, CHUNK), CHUNK)
        dmixed = grad_out_ref[0, :, cols].astype(F32) + rstd * (
            gin[:, cols] - m1 - nhat_ref[:, cols] * m2
        )
        grad_x_ref[0, :, cols] = dmixed.astype(BF16)
        values = jnp.concatenate(
            [(probs[:, 0:1] * dmixed).astype(BF16), (probs[:, 1:2] * dmixed).astype(BF16)], axis=0
        )
        placed = jnp.dot(hot, values, preferred_element_type=F32).astype(BF16)
        for e in range(group_count):
            out_refs[e][:, cols] = placed[e * slots : (e + 1) * slots]
        return (
            p0 + jnp.sum(dmixed * picked_ref[0, :, cols].astype(F32), axis=1, keepdims=True),
            p1 + jnp.sum(dmixed * picked_ref[1, :, cols].astype(F32), axis=1, keepdims=True),
        )

    p0, p1 = lax.fori_loop(0, chunks, back_step, (none, none))
    two = lax.broadcasted_iota(jnp.int32, (rows, 2), 1)
    grad_probs_ref[0] = jnp.where(two == 0, p0, p1)
    part = width // group_count
    for e in range(group_count):
        share = kacc[:, e * part : (e + 1) * part]
        if last_terms is not None:
            share = share + last_terms[e]
        terms_ref[e] = share


def whole(shape):
    return pl.BlockSpec(shape, lambda *_: (0,) * len(shape))


def of_micro(micro, shape):
    return pl.BlockSpec((1,) + shape[1:], lambda *_: (micro,) + (0,) * (len(shape) - 1))


def combine(micro, place, expert_out, tables, frames, flat, probs, gain):
    group_count = len(tables) + 1
    rows, width = frames.shape[1:]
    own = pl.BlockSpec(
        (None, None, 1) + expert_out.shape[3:],
        lambda _, place_ref: (micro, 0, place_ref[2], 0, 0, 0),
    )
    return pl.pallas_call(
        functools.partial(combine_kernel, group_count),
        grid_spec=pltpu.PrefetchScalarGridSpec(
            num_scalar_prefetch=1,
            grid=(1,),
            in_specs=[own]
            + [whole(t.shape) for t in tables]
            + [
                of_micro(micro, frames.shape),
                of_micro(micro, flat.shape),
                of_micro(micro, probs.shape),
                whole(gain.shape),
            ],
            out_specs=[
                whole((rows, width)),
                whole((2, SIDE, width)),
                whole((rows, width)),
                whole((rows, 128)),
                whole((2, rows, width)),
            ],
        ),
        out_shape=[
            jax.ShapeDtypeStruct((rows, width), BF16),
            jax.ShapeDtypeStruct((2, SIDE, width), BF16),
            jax.ShapeDtypeStruct((rows, width), F32),
            jax.ShapeDtypeStruct((rows, 128), F32),
            jax.ShapeDtypeStruct((2, rows, width), BF16),
        ],
        compiler_params=pltpu.CompilerParams(vmem_limit_bytes=VMEM_LIMIT),
        name="combine",
    )(place, expert_out, *tables, frames, flat, probs, gain)


def conv(micro, place, lengths, group_count, frame_total, conv_in, near, far, grad_out, gnear, gfar, nhat, rstd, picked, flat_row, probs, gain, kernel, earlier):
    rows, width = conv_in.shape
    micro_count = grad_out.shape[0]
    first = earlier is None
    slots = EXPERTS * CAP // group_count
    mid = rows + 2 * GSIDE
    full = rows + 2 * SIDE
    terms_shape = (group_count, KW + 1, width // group_count)
    in_specs = [
        whole(conv_in.shape),
        whole(near.shape),
        whole(far.shape),
        of_micro(micro, grad_out.shape),
        of_micro(micro, gnear.shape),
        of_micro(micro, gfar.shape),
        whole(nhat.shape),
        whole(rstd.shape),
        whole(picked.shape),
        of_micro(micro, flat_row.shape),
        of_micro(micro, probs.shape),
        whole(gain.shape),
        whole(kernel.shape),
    ]
    operands = [place, lengths, conv_in, near, far, grad_out, gnear, gfar, nhat, rstd, picked, flat_row, probs, gain, kernel]
    aliases = {}
    if not first:
        in_specs += [whole(terms_shape), pl.BlockSpec(memory_space=pl.ANY), pl.BlockSpec(memory_space=pl.ANY)]
        aliases = {len(operands) + 1: 0, len(operands) + 2: 1}
        operands += [earlier[2], earlier[0], earlier[1]]
    return pl.pallas_call(
        functools.partial(conv_kernel, group_count, first, micro, frame_total),
        grid_spec=pltpu.PrefetchScalarGridSpec(
            num_scalar_prefetch=2,
            grid=(1,),
            in_specs=in_specs,
            out_specs=[
                of_micro(micro, grad_out.shape),
                of_micro(micro, probs.shape),
                whole(terms_shape),
            ]
            + [whole((slots, width))] * group_count,
            scratch_shapes=[
                pltpu.VMEM((full, width), BF16),
                pltpu.VMEM((mid, width), BF16),
                pltpu.VMEM((KW * mid, full), BF16),
                pltpu.VMEM((full, CHUNK), BF16),
                pltpu.VMEM((rows, width), F32),
                pltpu.VMEM((KW + 1, width), F32),
            ],
        ),
        out_shape=[
            jax.ShapeDtypeStruct((micro_count, rows, width), BF16),
            jax.ShapeDtypeStruct(probs.shape, F32),
            jax.ShapeDtypeStruct(terms_shape, F32),
        ]
        + [jax.ShapeDtypeStruct((slots, width), BF16)] * group_count,
        input_output_aliases=aliases,
        compiler_params=pltpu.CompilerParams(vmem_limit_bytes=VMEM_LIMIT),
        name="conv",
    )(*operands)


def take(cells, index):
    return lax.dynamic_index_in_dim(cells, index, axis=0, keepdims=False)


def local(frames, expert_out, routes, order, probs, lengths, gain, kernel, grad_out):
    micro_count, rows, width = frames.shape
    groups = lax.axis_size("expert")
    tm = lax.axis_size("tm")
    both = ("tm", "expert")
    devices = groups * tm
    frame_total = rows * devices
    scale_norm = 1.0 / math.sqrt(micro_count * frame_total)
    me = lax.axis_index("expert")
    here = lax.axis_index(both)
    odd = lax.rem(here, 2)
    place = jnp.stack([here * rows, odd, me]).astype(jnp.int32)
    per = EXPERTS // groups
    block = per * CAP
    near_pairs = [(i, i ^ 1) for i in range(devices)]
    far_pairs = [(i, (i - 1) % devices if i % 2 == 0 else (i + 1) % devices) for i in range(devices)]

    def swap(cells, step):
        return lax.ppermute(cells, "expert", [(i, i ^ step) for i in range(groups)])

    tables = []
    for micro in range(micro_count):
        source = expert_out[micro, 0].reshape(groups, 1, block, width)
        tables.append([swap(take(source, me ^ step), step) for step in range(1, groups)])

    head, tail = grad_out[:, :GSIDE], grad_out[:, rows - GSIDE :]
    gnear = lax.ppermute(jnp.where(odd == 0, tail, head), both, near_pairs)
    gfar = lax.ppermute(jnp.where(odd == 0, head, tail), both, far_pairs)

    slots = jax.vmap(slot_table)(routes, order[:, 0])
    flat = ((routes // per) ^ me) * block + (routes % per) * CAP + slots
    flat_row = jnp.swapaxes(flat, 1, 2).reshape(micro_count, 1, 2 * rows)
    gain_row = gain[None, :]

    earlier = None
    returned = []
    for micro in range(micro_count):
        conv_in, sends, nhat, rstd, picked = combine(
            micro, place, expert_out, tables[micro], frames, flat, probs, gain_row
        )
        near = lax.ppermute(sends[0], both, near_pairs)
        far = lax.ppermute(sends[1], both, far_pairs)
        grad_x, grad_probs, terms, *outs = conv(
            micro, place, lengths, groups, frame_total, conv_in, near, far, grad_out, gnear, gfar,
            nhat, rstd, picked, flat_row, probs, gain_row, kernel, earlier,
        )
        earlier = (grad_x, grad_probs, terms)
        returned.append([outs[0]] + [swap(outs[step], step) for step in range(1, groups)])

    grad_expert = jnp.zeros((micro_count, groups, block, width), BF16)
    for micro in range(micro_count):
        for step in range(groups):
            grad_expert = lax.dynamic_update_slice(
                grad_expert, returned[micro][step][None, None], (micro, me ^ step, 0, 0)
            )
    grad_expert = grad_expert.reshape(micro_count, 1, groups, per, CAP, width)

    total = take(terms, me)
    for step in range(1, groups):
        total = total + swap(take(terms, me ^ step), step)
    step = 1
    while step < tm:
        total = total + lax.ppermute(total, "tm", [(i, i ^ step) for i in range(tm)])
        step *= 2
    total = total * scale_norm
    return grad_x, grad_expert, grad_probs, total[:KW], total[KW]


def solution(mesh):
    placed = (
        P(None, ("tm", "expert"), None),
        P(None, "tm", None, "expert", None, None),
        P(None, ("tm", "expert"), None),
        P(None, ("tm", "expert"), None),
        P(None, ("tm", "expert"), None),
        P(),
        P(),
        P(),
        P(None, ("tm", "expert"), None),
    )
    return jax.shard_map(
        local,
        mesh=mesh,
        in_specs=placed,
        out_specs=(
            P(None, ("tm", "expert"), None),
            P(None, "tm", None, "expert", None, None),
            P(None, ("tm", "expert"), None),
            P(None, "expert"),
            P("expert"),
        ),
        check_vma=False,
    )
```

```python
import functools
import math

import jax
import jax.numpy as jnp
from jax import lax
from jax.experimental import pallas as pl
from jax.experimental.pallas import tpu as pltpu
from jax.sharding import PartitionSpec as P

EXPERTS = 32
KW = 31
HALF = 15
CAP = 8
SIDE = 32
GSIDE = 16
F32 = jnp.float32
BF16 = jnp.bfloat16
VMEM_LIMIT = 12 * 1024 * 1024
SMALL_LIMIT = 4 * 1024 * 1024


def slot_table(route_rows, order_row):
    row_count = route_rows.shape[0]
    sort_keys = (order_row[:, None] * 2 + jnp.arange(2, dtype=jnp.int32)[None, :]).reshape(-1)
    owners = route_rows.reshape(-1)
    before = (owners[:, None] == owners[None, :]) & (sort_keys[None, :] < sort_keys[:, None])
    return jnp.sum(before.astype(jnp.int32), axis=1).reshape(row_count, 2)


def combine_kernel(
    group_count,
    place_ref,
    *rest,
):
    table_refs = rest[:group_count]
    frames_ref, grad_out_ref, flat_ref, probs_ref, gain_ref = rest[group_count : group_count + 5]
    conv_in_ref, near_ref, far_ref, nhat_ref, rstd_ref, picked_ref = rest[-6:]
    rows = frames_ref.shape[1]
    width = frames_ref.shape[2]
    flat = flat_ref[0]
    probs = probs_ref[0]
    table = jnp.concatenate([r[...] for r in table_refs], axis=0)
    lane = lax.broadcasted_iota(jnp.int32, (rows, table.shape[0]), 1)
    mixed = frames_ref[0].astype(F32)
    for k in range(2):
        hot = jnp.where(lane == flat[:, k : k + 1], 1.0, 0.0).astype(BF16)
        row = jnp.dot(hot, table, preferred_element_type=F32)
        picked_ref[k] = row.astype(BF16)
        mixed = mixed + probs[:, k : k + 1] * row
    mean = jnp.mean(mixed, axis=1, keepdims=True)
    centred = mixed - mean
    rstd = lax.rsqrt(jnp.mean(centred * centred, axis=1, keepdims=True) + 1e-05)
    nhat = centred * rstd
    nhat_ref[...] = nhat
    rstd_ref[...] = jnp.broadcast_to(rstd, rstd_ref.shape)
    conv_in = (nhat * gain_ref[...]).astype(BF16)
    conv_in_ref[...] = conv_in
    odd = place_ref[1]

    def send(ref, first):
        ref[:SIDE] = conv_in[:SIDE] if first else conv_in[rows - SIDE :]
        ref[SIDE:] = grad_out_ref[0, :GSIDE] if first else grad_out_ref[0, rows - GSIDE :]

    @pl.when(odd == 0)
    def _():
        send(near_ref, False)
        send(far_ref, True)

    @pl.when(odd == 1)
    def _():
        send(near_ref, True)
        send(far_ref, False)


def swish_slope(values):
    sigmoid_v = jax.nn.sigmoid(values)
    return sigmoid_v * (1.0 + values * (1.0 - sigmoid_v))


def conv_kernel(
    group_count,
    first,
    micro,
    frame_total,
    scale,
    place_ref,
    lengths_ref,
    conv_in_ref,
    near_ref,
    far_ref,
    grad_out_ref,
    nhat_ref,
    rstd_ref,
    picked_ref,
    flat_row_ref,
    probs_ref,
    gain_ref,
    kernel_ref,
    *rest,
):
    if first:
        grad_x_ref, grad_probs_ref, terms_ref = rest[:3]
        rest = rest[3:]
        last_terms = None
    else:
        last_terms, _, _, grad_x_ref, grad_probs_ref, terms_ref = rest[:6]
        rest = rest[6:]
    out_refs = rest[:group_count]
    window, gout, shifts, gwin, kacc = rest[group_count:]
    rows, width = conv_in_ref.shape
    mid = rows + 2 * GSIDE
    full = rows + 2 * SIDE
    odd = place_ref[1]

    window[SIDE : SIDE + rows, :] = conv_in_ref[...]
    gout[GSIDE : GSIDE + rows, :] = grad_out_ref[0]

    def receive(before, after):
        window[:SIDE, :] = before[:SIDE]
        window[SIDE + rows :, :] = after[:SIDE]
        gout[:GSIDE, :] = before[SIDE:]
        gout[GSIDE + rows :, :] = after[SIDE:]

    @pl.when(odd == 0)
    def _():
        receive(far_ref, near_ref)

    @pl.when(odd == 1)
    def _():
        receive(near_ref, far_ref)

    gwin[: SIDE - GSIDE, :] = jnp.zeros((SIDE - GSIDE, width), BF16)
    gwin[SIDE - GSIDE + mid :, :] = jnp.zeros((SIDE - GSIDE, width), BF16)

    first_frame = place_ref[0]
    t_local = lax.broadcasted_iota(jnp.int32, (mid, full), 0)
    r_local = lax.broadcasted_iota(jnp.int32, (mid, full), 1)
    t_pos = first_frame - GSIDE + t_local
    r_pos = first_frame - SIDE + r_local

    def count(u, carry):
        end, t_seg, r_seg = carry
        end = end + lengths_ref[micro, u]
        return (
            end,
            t_seg + jnp.where(t_pos >= end, 1, 0),
            r_seg + jnp.where(r_pos >= end, 1, 0),
        )

    zero = jnp.zeros((mid, full), jnp.int32)
    _, t_seg, r_seg = lax.fori_loop(0, lengths_ref.shape[1], count, (0, zero, zero))
    same = (t_seg == r_seg) & (t_pos >= 0) & (t_pos < frame_total) & (r_pos >= 0) & (r_pos < frame_total)
    gap = jnp.where(same, r_local - t_local - (SIDE - GSIDE - HALF), -1)
    for i in range(KW):
        shifts[i * mid : (i + 1) * mid, :] = jnp.where(gap == i, 1.0, 0.0).astype(BF16)

    taps = kernel_ref[...]
    xw = window[...]
    acc = jnp.zeros((mid, width), F32)
    for i in range(KW):
        v = jnp.dot(shifts[i * mid : (i + 1) * mid, :], xw, preferred_element_type=F32)
        acc = acc + taps[i : i + 1, :] * v
    g = (gout[...].astype(F32) * swish_slope(acc)).astype(BF16)
    gwin[SIDE - GSIDE : SIDE - GSIDE + mid, :] = g
    gw = gwin[...]
    x = conv_in_ref[...].astype(F32)
    acc = jnp.zeros((rows, width), F32)
    for j in range(KW):
        base = j * mid + GSIDE
        v = jnp.dot(shifts[base : base + rows, :], gw, preferred_element_type=F32)
        i = KW - 1 - j
        acc = acc + taps[i : i + 1, :] * v
        kacc[i : i + 1, :] = jnp.sum(x * v, axis=0, keepdims=True)
    grad_in = acc.astype(BF16).astype(F32)
    nhat = nhat_ref[...]
    kacc[KW : KW + 1, :] = jnp.sum(grad_in * nhat, axis=0, keepdims=True)
    dn = grad_in * gain_ref[...]
    m1 = jnp.sum(dn, axis=1, keepdims=True) * (1.0 / width)
    m2 = jnp.sum(dn * nhat, axis=1, keepdims=True) * (1.0 / width)
    rstd = rstd_ref[:, :1]
    dmixed = grad_out_ref[0].astype(F32) + rstd * (dn - m1 - nhat * m2)
    grad_x_ref[0] = dmixed.astype(BF16)
    probs = probs_ref[0]
    values = jnp.concatenate(
        [(probs[:, 0:1] * dmixed).astype(BF16), (probs[:, 1:2] * dmixed).astype(BF16)], axis=0
    )
    slots = out_refs[0].shape[0]
    spots = lax.broadcasted_iota(jnp.int32, (slots * group_count, 2 * rows), 0)
    hot = jnp.where(spots == flat_row_ref[0], 1.0, 0.0).astype(BF16)
    placed = jnp.dot(hot, values, preferred_element_type=F32).astype(BF16)
    for e in range(group_count):
        out_refs[e][...] = placed[e * slots : (e + 1) * slots]
    p0 = jnp.sum(dmixed * picked_ref[0].astype(F32), axis=1, keepdims=True)
    p1 = jnp.sum(dmixed * picked_ref[1].astype(F32), axis=1, keepdims=True)
    two = lax.broadcasted_iota(jnp.int32, (rows, 2), 1)
    grad_probs_ref[0] = jnp.where(two == 0, p0, p1)
    part = width // group_count
    for e in range(group_count):
        share = kacc[:, e * part : (e + 1) * part] * scale
        if last_terms is not None:
            share = share + last_terms[e]
        terms_ref[e] = share


def whole(shape):
    return pl.BlockSpec(shape, lambda *_: (0,) * len(shape))


def of_micro(micro, shape):
    return pl.BlockSpec((1,) + shape[1:], lambda *_: (micro,) + (0,) * (len(shape) - 1))


def combine(micro, place, tables, frames, grad_out, flat, probs, gain):
    group_count = len(tables)
    rows, width = frames.shape[1:]
    return pl.pallas_call(
        functools.partial(combine_kernel, group_count),
        grid_spec=pltpu.PrefetchScalarGridSpec(
            num_scalar_prefetch=1,
            grid=(1,),
            in_specs=[whole(t.shape) for t in tables]
            + [
                of_micro(micro, frames.shape),
                of_micro(micro, grad_out.shape),
                of_micro(micro, flat.shape),
                of_micro(micro, probs.shape),
                whole(gain.shape),
            ],
            out_specs=[
                whole((rows, width)),
                whole((SIDE + GSIDE, width)),
                whole((SIDE + GSIDE, width)),
                whole((rows, width)),
                whole((rows, 128)),
                whole((2, rows, width)),
            ],
        ),
        out_shape=[
            jax.ShapeDtypeStruct((rows, width), BF16),
            jax.ShapeDtypeStruct((SIDE + GSIDE, width), BF16),
            jax.ShapeDtypeStruct((SIDE + GSIDE, width), BF16),
            jax.ShapeDtypeStruct((rows, width), F32),
            jax.ShapeDtypeStruct((rows, 128), F32),
            jax.ShapeDtypeStruct((2, rows, width), BF16),
        ],
        compiler_params=pltpu.CompilerParams(vmem_limit_bytes=VMEM_LIMIT),
        cost_estimate=pl.CostEstimate(flops=1500 * 10**6, bytes_accessed=0, transcendentals=0),
        name="combine",
    )(place, *tables, frames, grad_out, flat, probs, gain)


def conv(micro, place, lengths, group_count, frame_total, conv_in, near, far, grad_out, nhat, rstd, picked, flat_row, probs, gain, kernel, earlier):
    rows, width = conv_in.shape
    micro_count = grad_out.shape[0]
    first = earlier is None
    slots = EXPERTS * CAP // group_count
    mid = rows + 2 * GSIDE
    full = rows + 2 * SIDE
    terms_shape = (group_count, KW + 1, width // group_count)
    in_specs = [
        whole(conv_in.shape),
        whole(near.shape),
        whole(far.shape),
        of_micro(micro, grad_out.shape),
        whole(nhat.shape),
        whole(rstd.shape),
        whole(picked.shape),
        of_micro(micro, flat_row.shape),
        of_micro(micro, probs.shape),
        whole(gain.shape),
        whole(kernel.shape),
    ]
    operands = [place, lengths, conv_in, near, far, grad_out, nhat, rstd, picked, flat_row, probs, gain, kernel]
    aliases = {}
    if not first:
        in_specs += [whole(terms_shape), pl.BlockSpec(memory_space=pl.ANY), pl.BlockSpec(memory_space=pl.ANY)]
        aliases = {len(operands) + 1: 0, len(operands) + 2: 1}
        operands += [earlier[2], earlier[0], earlier[1]]
    return pl.pallas_call(
        functools.partial(
            conv_kernel, group_count, first, micro, frame_total, 1.0 / math.sqrt(micro_count * frame_total)
        ),
        grid_spec=pltpu.PrefetchScalarGridSpec(
            num_scalar_prefetch=2,
            grid=(1,),
            in_specs=in_specs,
            out_specs=[
                of_micro(micro, grad_out.shape),
                of_micro(micro, probs.shape),
                whole(terms_shape),
            ]
            + [whole((slots, width))] * group_count,
            scratch_shapes=[
                pltpu.VMEM((full, width), BF16),
                pltpu.VMEM((mid, width), BF16),
                pltpu.VMEM((KW * mid, full), BF16),
                pltpu.VMEM((full, width), BF16),
                pltpu.VMEM((KW + 1, width), F32),
            ],
        ),
        out_shape=[
            jax.ShapeDtypeStruct((micro_count, rows, width), BF16),
            jax.ShapeDtypeStruct(probs.shape, F32),
            jax.ShapeDtypeStruct(terms_shape, F32),
        ]
        + [jax.ShapeDtypeStruct((slots, width), BF16)] * group_count,
        input_output_aliases=aliases,
        compiler_params=pltpu.CompilerParams(vmem_limit_bytes=VMEM_LIMIT),
        cost_estimate=pl.CostEstimate(flops=8 * 10**9, bytes_accessed=0, transcendentals=0),
        name="conv",
    )(*operands)


def finish_kernel(group_count, micro, part_count, place_ref, *refs):
    blocks = refs[:group_count]
    parts = refs[group_count : group_count + part_count]
    rest = refs[group_count + part_count :]
    if part_count:
        _, out_ref, taps_ref, gain_ref, sems = rest
    else:
        out_ref, sems = rest
    me = place_ref[2]
    copies = [
        pltpu.make_async_copy(block, out_ref.at[micro, jnp.bitwise_xor(me, step)], sems.at[step])
        for step, block in enumerate(blocks)
    ]
    for copy in copies:
        copy.start()
    if part_count:
        total = parts[0][...]
        for part in parts[1:]:
            total = total + part[...]
        taps_ref[...] = total[:KW]
        gain_ref[...] = total[KW]
    for copy in copies:
        copy.wait()


def finish(micro, micro_count, place, blocks, parts=(), earlier=None):
    group_count = len(blocks)
    slots, width = blocks[0].shape
    anywhere = pl.BlockSpec(memory_space=pl.ANY)
    out_shape = [jax.ShapeDtypeStruct((micro_count, group_count, slots, width), BF16)]
    out_specs = [anywhere]
    in_specs = [anywhere] * group_count + [whole(p.shape) for p in parts]
    operands = [place, *blocks, *parts]
    aliases = {}
    if earlier is not None:
        aliases = {len(operands): 0}
        operands.append(earlier)
        in_specs.append(anywhere)
        share = parts[0].shape[1]
        out_shape += [jax.ShapeDtypeStruct((KW, share), F32), jax.ShapeDtypeStruct((share,), F32)]
        out_specs += [whole((KW, share)), whole((share,))]
    return pl.pallas_call(
        functools.partial(finish_kernel, group_count, micro, len(parts)),
        grid_spec=pltpu.PrefetchScalarGridSpec(
            num_scalar_prefetch=1,
            grid=(1,),
            in_specs=in_specs,
            out_specs=out_specs,
            scratch_shapes=[pltpu.SemaphoreType.DMA((group_count,))],
        ),
        out_shape=out_shape,
        input_output_aliases=aliases,
        compiler_params=pltpu.CompilerParams(vmem_limit_bytes=4 * 1024 * 1024),
        cost_estimate=pl.CostEstimate(flops=1000 * 10**6, bytes_accessed=0, transcendentals=0),
        name="finish",
    )(*operands)


def take(cells, index):
    return lax.dynamic_index_in_dim(cells, index, axis=0, keepdims=False)


def local(frames, expert_out, routes, order, probs, lengths, gain, kernel, grad_out):
    micro_count, rows, width = frames.shape
    groups = lax.axis_size("expert")
    tm = lax.axis_size("tm")
    both = ("tm", "expert")
    devices = groups * tm
    frame_total = rows * devices
    me = lax.axis_index("expert")
    here = lax.axis_index(both)
    odd = lax.rem(here, 2)
    place = jnp.stack([here * rows, odd, me]).astype(jnp.int32)
    per = EXPERTS // groups
    block = per * CAP
    near_pairs = [(i, i ^ 1) for i in range(devices)]
    far_pairs = [(i, (i - 1) % devices if i % 2 == 0 else (i + 1) % devices) for i in range(devices)]

    def swap(cells, step):
        return lax.ppermute(cells, "expert", [(i, i ^ step) for i in range(groups)])

    tables = []
    cells = expert_out
    sizes = (1, 1, 1) + expert_out.shape[3:]
    for micro in range(micro_count):
        blocks = [
            lax.dynamic_slice(cells, (micro, 0, me ^ step, 0, 0, 0), sizes).reshape(block, width)
            for step in range(groups)
        ]
        cells, *blocks = lax.optimization_barrier([cells, *blocks])
        tables.append([blocks[0]] + [swap(blocks[step], step) for step in range(1, groups)])

    slots = jax.vmap(slot_table)(routes, order[:, 0])
    flat = ((routes // per) ^ me) * block + (routes % per) * CAP + slots
    flat_row = jnp.swapaxes(flat, 1, 2).reshape(micro_count, 1, 2 * rows)
    gain_row = gain[None, :]

    earlier = None
    returned = []
    for micro in range(micro_count):
        conv_in, near, far, nhat, rstd, picked = combine(
            micro, place, tables[micro], frames, grad_out, flat, probs, gain_row
        )
        near = lax.ppermute(near, both, near_pairs)
        far = lax.ppermute(far, both, far_pairs)
        grad_x, grad_probs, terms, *outs = conv(
            micro, place, lengths, groups, frame_total, conv_in, near, far, grad_out,
            nhat, rstd, picked, flat_row, probs, gain_row, kernel, earlier,
        )
        earlier = (grad_x, grad_probs, terms)
        if returned:
            returned[-1], outs = lax.optimization_barrier((returned[-1], outs))
        returned.append([outs[0]] + [swap(outs[step], step) for step in range(1, groups)])

    def over(cells, steps):
        return [lax.ppermute(cells, "tm", [(i, i ^ step) for i in range(tm)]) for step in steps]

    total = take(terms, me)
    for step in range(1, groups):
        total = total + swap(take(terms, me ^ step), step)
    step = 1
    while step < tm // 2:
        total = total + over(total, [step])[0]
        step *= 2
    parts = [total] + over(total, [step])
    grad_expert = None
    for micro in range(micro_count - 1):
        (grad_expert,) = finish(micro, micro_count, place, returned[micro])
    grad_expert, grad_kernel, grad_gain = finish(
        micro_count - 1, micro_count, place, returned[-1], parts, grad_expert
    )
    grad_expert = grad_expert.reshape(micro_count, 1, groups, per, CAP, width)
    return grad_x, grad_expert, grad_probs, grad_kernel, grad_gain


def solution(mesh):
    placed = (
        P(None, ("tm", "expert"), None),
        P(None, "tm", None, "expert", None, None),
        P(None, ("tm", "expert"), None),
        P(None, ("tm", "expert"), None),
        P(None, ("tm", "expert"), None),
        P(),
        P(),
        P(),
        P(None, ("tm", "expert"), None),
    )
    return jax.shard_map(
        local,
        mesh=mesh,
        in_specs=placed,
        out_specs=(
            P(None, ("tm", "expert"), None),
            P(None, "tm", None, "expert", None, None),
            P(None, ("tm", "expert"), None),
            P(None, "expert"),
            P("expert"),
        ),
        check_vma=False,
    )
```

```python
import functools
import math

import jax
import jax.numpy as jnp
from jax import lax
from jax.experimental import pallas as pl
from jax.experimental.pallas import tpu as pltpu
from jax.sharding import PartitionSpec as P

EXPERTS = 32
KW = 31
HALF = 15
CAP = 8
SIDE = 32
GSIDE = 16
F32 = jnp.float32
BF16 = jnp.bfloat16
VMEM_LIMIT = 12 * 1024 * 1024
SMALL_LIMIT = 4 * 1024 * 1024


def slot_table(route_rows, order_row):
    row_count = route_rows.shape[0]
    sort_keys = (order_row[:, None] * 2 + jnp.arange(2, dtype=jnp.int32)[None, :]).reshape(-1)
    owners = route_rows.reshape(-1)
    before = (owners[:, None] == owners[None, :]) & (sort_keys[None, :] < sort_keys[:, None])
    return jnp.sum(before.astype(jnp.int32), axis=1).reshape(row_count, 2)


def combine_kernel(
    group_count,
    place_ref,
    *rest,
):
    table_refs = rest[:group_count]
    frames_ref, grad_out_ref, flat_ref, probs_ref, gain_ref = rest[group_count : group_count + 5]
    conv_in_ref, near_ref, far_ref, nhat_ref, rstd_ref, picked_ref = rest[-6:]
    rows = frames_ref.shape[1]
    width = frames_ref.shape[2]
    flat = flat_ref[0]
    probs = probs_ref[0]
    table = jnp.concatenate([r[...] for r in table_refs], axis=0)
    lane = lax.broadcasted_iota(jnp.int32, (rows, table.shape[0]), 1)
    mixed = frames_ref[0].astype(F32)
    for k in range(2):
        hot = jnp.where(lane == flat[:, k : k + 1], 1.0, 0.0).astype(BF16)
        row = jnp.dot(hot, table, preferred_element_type=F32)
        picked_ref[k] = row.astype(BF16)
        mixed = mixed + probs[:, k : k + 1] * row
    mean = jnp.mean(mixed, axis=1, keepdims=True)
    centred = mixed - mean
    rstd = lax.rsqrt(jnp.mean(centred * centred, axis=1, keepdims=True) + 1e-05)
    nhat = centred * rstd
    nhat_ref[...] = nhat
    rstd_ref[...] = jnp.broadcast_to(rstd, rstd_ref.shape)
    conv_in = (nhat * gain_ref[...]).astype(BF16)
    conv_in_ref[...] = conv_in
    odd = place_ref[1]

    def send(ref, first):
        ref[:SIDE] = conv_in[:SIDE] if first else conv_in[rows - SIDE :]
        ref[SIDE:] = grad_out_ref[0, :GSIDE] if first else grad_out_ref[0, rows - GSIDE :]

    @pl.when(odd == 0)
    def _():
        send(near_ref, False)
        send(far_ref, True)

    @pl.when(odd == 1)
    def _():
        send(near_ref, True)
        send(far_ref, False)


def swish_slope(values):
    sigmoid_v = jax.nn.sigmoid(values)
    return sigmoid_v * (1.0 + values * (1.0 - sigmoid_v))


def conv_kernel(
    group_count,
    first,
    micro,
    frame_total,
    scale,
    place_ref,
    lengths_ref,
    conv_in_ref,
    near_ref,
    far_ref,
    grad_out_ref,
    nhat_ref,
    rstd_ref,
    picked_ref,
    flat_row_ref,
    probs_ref,
    gain_ref,
    kernel_ref,
    *rest,
):
    if first:
        grad_x_ref, grad_probs_ref, terms_ref = rest[:3]
        rest = rest[3:]
        last_terms = None
    else:
        last_terms, _, _, grad_x_ref, grad_probs_ref, terms_ref = rest[:6]
        rest = rest[6:]
    out_refs = rest[:group_count]
    window, gout, shifts, gwin, kacc = rest[group_count:]
    rows, width = conv_in_ref.shape
    mid = rows + 2 * GSIDE
    full = rows + 2 * SIDE
    odd = place_ref[1]

    window[SIDE : SIDE + rows, :] = conv_in_ref[...]
    gout[GSIDE : GSIDE + rows, :] = grad_out_ref[0]

    def receive(before, after):
        window[:SIDE, :] = before[:SIDE]
        window[SIDE + rows :, :] = after[:SIDE]
        gout[:GSIDE, :] = before[SIDE:]
        gout[GSIDE + rows :, :] = after[SIDE:]

    @pl.when(odd == 0)
    def _():
        receive(far_ref, near_ref)

    @pl.when(odd == 1)
    def _():
        receive(near_ref, far_ref)

    gwin[: SIDE - GSIDE, :] = jnp.zeros((SIDE - GSIDE, width), BF16)
    gwin[SIDE - GSIDE + mid :, :] = jnp.zeros((SIDE - GSIDE, width), BF16)

    first_frame = place_ref[0]
    t_local = lax.broadcasted_iota(jnp.int32, (mid, full), 0)
    r_local = lax.broadcasted_iota(jnp.int32, (mid, full), 1)
    t_pos = first_frame - GSIDE + t_local
    r_pos = first_frame - SIDE + r_local

    def count(u, carry):
        end, t_seg, r_seg = carry
        end = end + lengths_ref[micro, u]
        return (
            end,
            t_seg + jnp.where(t_pos >= end, 1, 0),
            r_seg + jnp.where(r_pos >= end, 1, 0),
        )

    zero = jnp.zeros((mid, full), jnp.int32)
    _, t_seg, r_seg = lax.fori_loop(0, lengths_ref.shape[1], count, (0, zero, zero))
    same = (t_seg == r_seg) & (t_pos >= 0) & (t_pos < frame_total) & (r_pos >= 0) & (r_pos < frame_total)
    gap = jnp.where(same, r_local - t_local - (SIDE - GSIDE - HALF), -1)
    for i in range(KW):
        shifts[i * mid : (i + 1) * mid, :] = jnp.where(gap == i, 1.0, 0.0).astype(BF16)

    taps = kernel_ref[...]
    xw = window[...]
    acc = jnp.zeros((mid, width), F32)
    for i in range(KW):
        v = jnp.dot(shifts[i * mid : (i + 1) * mid, :], xw, preferred_element_type=F32)
        acc = acc + taps[i : i + 1, :] * v
    g = (gout[...].astype(F32) * swish_slope(acc)).astype(BF16)
    gwin[SIDE - GSIDE : SIDE - GSIDE + mid, :] = g
    gw = gwin[...]
    x = conv_in_ref[...].astype(F32)
    acc = jnp.zeros((rows, width), F32)
    for j in range(KW):
        base = j * mid + GSIDE
        v = jnp.dot(shifts[base : base + rows, :], gw, preferred_element_type=F32)
        i = KW - 1 - j
        acc = acc + taps[i : i + 1, :] * v
        kacc[i : i + 1, :] = jnp.sum(x * v, axis=0, keepdims=True)
    grad_in = acc.astype(BF16).astype(F32)
    nhat = nhat_ref[...]
    kacc[KW : KW + 1, :] = jnp.sum(grad_in * nhat, axis=0, keepdims=True)
    dn = grad_in * gain_ref[...]
    m1 = jnp.sum(dn, axis=1, keepdims=True) * (1.0 / width)
    m2 = jnp.sum(dn * nhat, axis=1, keepdims=True) * (1.0 / width)
    rstd = rstd_ref[:, :1]
    dmixed = grad_out_ref[0].astype(F32) + rstd * (dn - m1 - nhat * m2)
    grad_x_ref[0] = dmixed.astype(BF16)
    probs = probs_ref[0]
    values = jnp.concatenate(
        [(probs[:, 0:1] * dmixed).astype(BF16), (probs[:, 1:2] * dmixed).astype(BF16)], axis=0
    )
    slots = out_refs[0].shape[0]
    spots = lax.broadcasted_iota(jnp.int32, (slots * group_count, 2 * rows), 0)
    hot = jnp.where(spots == flat_row_ref[0], 1.0, 0.0).astype(BF16)
    placed = jnp.dot(hot, values, preferred_element_type=F32).astype(BF16)
    for e in range(group_count):
        out_refs[e][...] = placed[e * slots : (e + 1) * slots]
    p0 = jnp.sum(dmixed * picked_ref[0].astype(F32), axis=1, keepdims=True)
    p1 = jnp.sum(dmixed * picked_ref[1].astype(F32), axis=1, keepdims=True)
    two = lax.broadcasted_iota(jnp.int32, (rows, 2), 1)
    grad_probs_ref[0] = jnp.where(two == 0, p0, p1)
    part = width // group_count
    for e in range(group_count):
        share = kacc[:, e * part : (e + 1) * part] * scale
        if last_terms is not None:
            share = share + last_terms[e]
        terms_ref[e] = share


def whole(shape):
    return pl.BlockSpec(shape, lambda *_: (0,) * len(shape))


def of_micro(micro, shape):
    return pl.BlockSpec((1,) + shape[1:], lambda *_: (micro,) + (0,) * (len(shape) - 1))


def combine(micro, place, tables, frames, grad_out, flat, probs, gain):
    group_count = len(tables)
    rows, width = frames.shape[1:]
    return pl.pallas_call(
        functools.partial(combine_kernel, group_count),
        grid_spec=pltpu.PrefetchScalarGridSpec(
            num_scalar_prefetch=1,
            grid=(1,),
            in_specs=[whole(t.shape) for t in tables]
            + [
                of_micro(micro, frames.shape),
                of_micro(micro, grad_out.shape),
                of_micro(micro, flat.shape),
                of_micro(micro, probs.shape),
                whole(gain.shape),
            ],
            out_specs=[
                whole((rows, width)),
                whole((SIDE + GSIDE, width)),
                whole((SIDE + GSIDE, width)),
                whole((rows, width)),
                whole((rows, 128)),
                whole((2, rows, width)),
            ],
        ),
        out_shape=[
            jax.ShapeDtypeStruct((rows, width), BF16),
            jax.ShapeDtypeStruct((SIDE + GSIDE, width), BF16),
            jax.ShapeDtypeStruct((SIDE + GSIDE, width), BF16),
            jax.ShapeDtypeStruct((rows, width), F32),
            jax.ShapeDtypeStruct((rows, 128), F32),
            jax.ShapeDtypeStruct((2, rows, width), BF16),
        ],
        compiler_params=pltpu.CompilerParams(vmem_limit_bytes=VMEM_LIMIT),
        cost_estimate=pl.CostEstimate(flops=1500 * 10**6, bytes_accessed=0, transcendentals=0),
        name="combine",
    )(place, *tables, frames, grad_out, flat, probs, gain)


def conv(micro, place, lengths, group_count, frame_total, conv_in, near, far, grad_out, nhat, rstd, picked, flat_row, probs, gain, kernel, earlier):
    rows, width = conv_in.shape
    micro_count = grad_out.shape[0]
    first = earlier is None
    slots = EXPERTS * CAP // group_count
    mid = rows + 2 * GSIDE
    full = rows + 2 * SIDE
    terms_shape = (group_count, KW + 1, width // group_count)
    in_specs = [
        whole(conv_in.shape),
        whole(near.shape),
        whole(far.shape),
        of_micro(micro, grad_out.shape),
        whole(nhat.shape),
        whole(rstd.shape),
        whole(picked.shape),
        of_micro(micro, flat_row.shape),
        of_micro(micro, probs.shape),
        whole(gain.shape),
        whole(kernel.shape),
    ]
    operands = [place, lengths, conv_in, near, far, grad_out, nhat, rstd, picked, flat_row, probs, gain, kernel]
    aliases = {}
    if not first:
        in_specs += [whole(terms_shape), pl.BlockSpec(memory_space=pl.ANY), pl.BlockSpec(memory_space=pl.ANY)]
        aliases = {len(operands) + 1: 0, len(operands) + 2: 1}
        operands += [earlier[2], earlier[0], earlier[1]]
    return pl.pallas_call(
        functools.partial(
            conv_kernel, group_count, first, micro, frame_total, 1.0 / math.sqrt(micro_count * frame_total)
        ),
        grid_spec=pltpu.PrefetchScalarGridSpec(
            num_scalar_prefetch=2,
            grid=(1,),
            in_specs=in_specs,
            out_specs=[
                of_micro(micro, grad_out.shape),
                of_micro(micro, probs.shape),
                whole(terms_shape),
            ]
            + [whole((slots, width))] * group_count,
            scratch_shapes=[
                pltpu.VMEM((full, width), BF16),
                pltpu.VMEM((mid, width), BF16),
                pltpu.VMEM((KW * mid, full), BF16),
                pltpu.VMEM((full, width), BF16),
                pltpu.VMEM((KW + 1, width), F32),
            ],
        ),
        out_shape=[
            jax.ShapeDtypeStruct((micro_count, rows, width), BF16),
            jax.ShapeDtypeStruct(probs.shape, F32),
            jax.ShapeDtypeStruct(terms_shape, F32),
        ]
        + [jax.ShapeDtypeStruct((slots, width), BF16)] * group_count,
        input_output_aliases=aliases,
        compiler_params=pltpu.CompilerParams(vmem_limit_bytes=VMEM_LIMIT),
        cost_estimate=pl.CostEstimate(flops=8 * 10**9, bytes_accessed=0, transcendentals=0),
        name="conv",
    )(*operands)


def finish_kernel(group_count, micro, place_ref, *refs):
    blocks = refs[:group_count]
    out_ref, sems = refs[-2:]
    me = place_ref[2]
    copies = [
        pltpu.make_async_copy(block, out_ref.at[micro, jnp.bitwise_xor(me, step)], sems.at[step])
        for step, block in enumerate(blocks)
    ]
    for copy in copies:
        copy.start()
    for copy in copies:
        copy.wait()


def finish(micro, micro_count, place, blocks, earlier=None):
    group_count = len(blocks)
    slots, width = blocks[0].shape
    anywhere = pl.BlockSpec(memory_space=pl.ANY)
    operands = [place, *blocks]
    aliases = {}
    if earlier is not None:
        aliases = {len(operands): 0}
        operands.append(earlier)
    return pl.pallas_call(
        functools.partial(finish_kernel, group_count, micro),
        in_specs=[pl.BlockSpec(memory_space=pltpu.SMEM)] + [anywhere] * (len(operands) - 1),
        out_specs=anywhere,
        out_shape=jax.ShapeDtypeStruct((micro_count, group_count, slots, width), BF16),
        scratch_shapes=[pltpu.SemaphoreType.DMA((group_count,))],
        input_output_aliases=aliases,
        compiler_params=pltpu.CompilerParams(vmem_limit_bytes=SMALL_LIMIT),
        cost_estimate=pl.CostEstimate(flops=1500 * 10**6, bytes_accessed=0, transcendentals=0),
        name="finish",
    )(*operands)


def total_kernel(*refs):
    parts = refs[:-2]
    taps_ref, gain_ref = refs[-2:]
    total = parts[0][...]
    for part in parts[1:]:
        total = total + part[...]
    taps_ref[...] = total[:KW]
    gain_ref[...] = total[KW]


def total_of(parts):
    share = parts[0].shape[1]
    inside = pl.BlockSpec(memory_space=pltpu.VMEM)
    return pl.pallas_call(
        total_kernel,
        in_specs=[inside] * len(parts),
        out_specs=[inside, inside],
        out_shape=[jax.ShapeDtypeStruct((KW, share), F32), jax.ShapeDtypeStruct((share,), F32)],
        compiler_params=pltpu.CompilerParams(vmem_limit_bytes=SMALL_LIMIT),
        name="total",
    )(*parts)


def take(cells, index):
    return lax.dynamic_index_in_dim(cells, index, axis=0, keepdims=False)


def local(frames, expert_out, routes, order, probs, lengths, gain, kernel, grad_out):
    micro_count, rows, width = frames.shape
    groups = lax.axis_size("expert")
    tm = lax.axis_size("tm")
    both = ("tm", "expert")
    devices = groups * tm
    frame_total = rows * devices
    me = lax.axis_index("expert")
    here = lax.axis_index(both)
    odd = lax.rem(here, 2)
    place = jnp.stack([here * rows, odd, me]).astype(jnp.int32)
    per = EXPERTS // groups
    block = per * CAP
    near_pairs = [(i, i ^ 1) for i in range(devices)]
    far_pairs = [(i, (i - 1) % devices if i % 2 == 0 else (i + 1) % devices) for i in range(devices)]

    def swap(cells, step):
        return lax.ppermute(cells, "expert", [(i, i ^ step) for i in range(groups)])

    tables = []
    cells = expert_out
    sizes = (1, 1, 1) + expert_out.shape[3:]
    for micro in range(micro_count):
        blocks = [
            lax.dynamic_slice(cells, (micro, 0, me ^ step, 0, 0, 0), sizes).reshape(block, width)
            for step in range(groups)
        ]
        cells, *blocks = lax.optimization_barrier([cells, *blocks])
        tables.append([blocks[0]] + [swap(blocks[step], step) for step in range(1, groups)])

    slots = jax.vmap(slot_table)(routes, order[:, 0])
    flat = ((routes // per) ^ me) * block + (routes % per) * CAP + slots
    flat_row = jnp.swapaxes(flat, 1, 2).reshape(micro_count, 1, 2 * rows)
    gain_row = gain[None, :]

    earlier = None
    returned = []
    for micro in range(micro_count):
        conv_in, near, far, nhat, rstd, picked = combine(
            micro, place, tables[micro], frames, grad_out, flat, probs, gain_row
        )
        near = lax.ppermute(near, both, near_pairs)
        far = lax.ppermute(far, both, far_pairs)
        grad_x, grad_probs, terms, *outs = conv(
            micro, place, lengths, groups, frame_total, conv_in, near, far, grad_out,
            nhat, rstd, picked, flat_row, probs, gain_row, kernel, earlier,
        )
        earlier = (grad_x, grad_probs, terms)
        if returned:
            returned[-1][:2], terms = lax.optimization_barrier((returned[-1][:2], terms))
            returned[-1], outs = lax.optimization_barrier((returned[-1], outs))
        returned.append([outs[0]] + [swap(outs[step], step) for step in range(1, groups)])

    def over(cells, steps):
        return [lax.ppermute(cells, "tm", [(i, i ^ step) for i in range(tm)]) for step in steps]

    total = take(terms, me)
    for step in range(1, groups):
        total = total + swap(take(terms, me ^ step), step)
    step = 1
    while step < tm // 2:
        total = total + over(total, [step])[0]
        step *= 2
    parts = [total] + over(total, [step])
    grad_expert = None
    for micro in range(micro_count):
        grad_expert = finish(micro, micro_count, place, returned[micro], grad_expert)
    grad_kernel, grad_gain = total_of(parts)
    grad_expert = grad_expert.reshape(micro_count, 1, groups, per, CAP, width)
    return grad_x, grad_expert, grad_probs, grad_kernel, grad_gain


def solution(mesh):
    placed = (
        P(None, ("tm", "expert"), None),
        P(None, "tm", None, "expert", None, None),
        P(None, ("tm", "expert"), None),
        P(None, ("tm", "expert"), None),
        P(None, ("tm", "expert"), None),
        P(),
        P(),
        P(),
        P(None, ("tm", "expert"), None),
    )
    return jax.shard_map(
        local,
        mesh=mesh,
        in_specs=placed,
        out_specs=(
            P(None, ("tm", "expert"), None),
            P(None, "tm", None, "expert", None, None),
            P(None, ("tm", "expert"), None),
            P(None, "expert"),
            P("expert"),
        ),
        check_vma=False,
    )
```

```python
import functools
import math

import jax
import jax.numpy as jnp
from jax import lax
from jax.experimental import pallas as pl
from jax.experimental.pallas import tpu as pltpu
from jax.sharding import PartitionSpec as P

EXPERTS = 32
KW = 31
HALF = 15
CAP = 8
SIDE = 32
GSIDE = 16
F32 = jnp.float32
BF16 = jnp.bfloat16
VMEM_LIMIT = 12 * 1024 * 1024
SMALL_LIMIT = 4 * 1024 * 1024


def slot_table(route_rows, order_row):
    row_count = route_rows.shape[0]
    sort_keys = (order_row[:, None] * 2 + jnp.arange(2, dtype=jnp.int32)[None, :]).reshape(-1)
    owners = route_rows.reshape(-1)
    before = (owners[:, None] == owners[None, :]) & (sort_keys[None, :] < sort_keys[:, None])
    return jnp.sum(before.astype(jnp.int32), axis=1).reshape(row_count, 2)


def combine_kernel(
    group_count,
    place_ref,
    *rest,
):
    table_refs = rest[:group_count]
    frames_ref, grad_out_ref, flat_ref, probs_ref, gain_ref = rest[group_count : group_count + 5]
    near_ref, far_ref, nhat_ref, rstd_ref, picked_ref = rest[-5:]
    rows = frames_ref.shape[1]
    width = frames_ref.shape[2]
    flat = flat_ref[0]
    probs = probs_ref[0]
    table = jnp.concatenate([r[...] for r in table_refs], axis=0)
    lane = lax.broadcasted_iota(jnp.int32, (rows, table.shape[0]), 1)
    mixed = frames_ref[0].astype(F32)
    for k in range(2):
        hot = jnp.where(lane == flat[:, k : k + 1], 1.0, 0.0).astype(BF16)
        row = jnp.dot(hot, table, preferred_element_type=F32)
        picked_ref[k] = row.astype(BF16)
        mixed = mixed + probs[:, k : k + 1] * row
    mean = jnp.mean(mixed, axis=1, keepdims=True)
    centred = mixed - mean
    rstd = lax.rsqrt(jnp.mean(centred * centred, axis=1, keepdims=True) + 1e-05)
    nhat = centred * rstd
    nhat_ref[...] = nhat
    rstd_ref[...] = jnp.broadcast_to(rstd, rstd_ref.shape)
    conv_in = (nhat * gain_ref[...]).astype(BF16)
    odd = place_ref[1]

    def send(ref, first):
        ref[:SIDE] = conv_in[:SIDE] if first else conv_in[rows - SIDE :]
        ref[SIDE:] = grad_out_ref[0, :GSIDE] if first else grad_out_ref[0, rows - GSIDE :]

    @pl.when(odd == 0)
    def _():
        send(near_ref, False)
        send(far_ref, True)

    @pl.when(odd == 1)
    def _():
        send(near_ref, True)
        send(far_ref, False)


def swish_slope(values):
    sigmoid_v = jax.nn.sigmoid(values)
    return sigmoid_v * (1.0 + values * (1.0 - sigmoid_v))


def conv_kernel(
    group_count,
    first,
    micro,
    frame_total,
    scale,
    place_ref,
    lengths_ref,
    near_ref,
    far_ref,
    grad_out_ref,
    nhat_ref,
    rstd_ref,
    picked_ref,
    flat_row_ref,
    probs_ref,
    gain_ref,
    kernel_ref,
    *rest,
):
    if first:
        grad_x_ref, grad_probs_ref, terms_ref = rest[:3]
        rest = rest[3:]
        last_terms = None
    else:
        last_terms, _, _, grad_x_ref, grad_probs_ref, terms_ref = rest[:6]
        rest = rest[6:]
    out_refs = rest[:group_count]
    window, gout, shifts, gwin, kacc = rest[group_count:]
    rows, width = nhat_ref.shape
    conv_in = (nhat_ref[...] * gain_ref[...]).astype(BF16)
    mid = rows + 2 * GSIDE
    full = rows + 2 * SIDE
    odd = place_ref[1]

    window[SIDE : SIDE + rows, :] = conv_in
    gout[GSIDE : GSIDE + rows, :] = grad_out_ref[0]

    def receive(before, after):
        window[:SIDE, :] = before[:SIDE]
        window[SIDE + rows :, :] = after[:SIDE]
        gout[:GSIDE, :] = before[SIDE:]
        gout[GSIDE + rows :, :] = after[SIDE:]

    @pl.when(odd == 0)
    def _():
        receive(far_ref, near_ref)

    @pl.when(odd == 1)
    def _():
        receive(near_ref, far_ref)

    gwin[: SIDE - GSIDE, :] = jnp.zeros((SIDE - GSIDE, width), BF16)
    gwin[SIDE - GSIDE + mid :, :] = jnp.zeros((SIDE - GSIDE, width), BF16)

    first_frame = place_ref[0]
    t_local = lax.broadcasted_iota(jnp.int32, (mid, full), 0)
    r_local = lax.broadcasted_iota(jnp.int32, (mid, full), 1)
    t_pos = first_frame - GSIDE + t_local
    r_pos = first_frame - SIDE + r_local

    def count(u, carry):
        end, t_seg, r_seg = carry
        end = end + lengths_ref[micro, u]
        return (
            end,
            t_seg + jnp.where(t_pos >= end, 1, 0),
            r_seg + jnp.where(r_pos >= end, 1, 0),
        )

    zero = jnp.zeros((mid, full), jnp.int32)
    _, t_seg, r_seg = lax.fori_loop(0, lengths_ref.shape[1], count, (0, zero, zero))
    same = (t_seg == r_seg) & (t_pos >= 0) & (t_pos < frame_total) & (r_pos >= 0) & (r_pos < frame_total)
    gap = jnp.where(same, r_local - t_local - (SIDE - GSIDE - HALF), -1)
    for i in range(KW):
        shifts[i * mid : (i + 1) * mid, :] = jnp.where(gap == i, 1.0, 0.0).astype(BF16)

    taps = kernel_ref[...]
    xw = window[...]
    acc = jnp.zeros((mid, width), F32)
    for i in range(KW):
        v = jnp.dot(shifts[i * mid : (i + 1) * mid, :], xw, preferred_element_type=F32)
        acc = acc + taps[i : i + 1, :] * v
    g = (gout[...].astype(F32) * swish_slope(acc)).astype(BF16)
    gwin[SIDE - GSIDE : SIDE - GSIDE + mid, :] = g
    gw = gwin[...]
    x = conv_in.astype(F32)
    acc = jnp.zeros((rows, width), F32)
    for j in range(KW):
        base = j * mid + GSIDE
        v = jnp.dot(shifts[base : base + rows, :], gw, preferred_element_type=F32)
        i = KW - 1 - j
        acc = acc + taps[i : i + 1, :] * v
        kacc[i : i + 1, :] = jnp.sum(x * v, axis=0, keepdims=True)
    grad_in = acc.astype(BF16).astype(F32)
    nhat = nhat_ref[...]
    kacc[KW : KW + 1, :] = jnp.sum(grad_in * nhat, axis=0, keepdims=True)
    dn = grad_in * gain_ref[...]
    m1 = jnp.sum(dn, axis=1, keepdims=True) * (1.0 / width)
    m2 = jnp.sum(dn * nhat, axis=1, keepdims=True) * (1.0 / width)
    rstd = rstd_ref[:, :1]
    dmixed = grad_out_ref[0].astype(F32) + rstd * (dn - m1 - nhat * m2)
    grad_x_ref[0] = dmixed.astype(BF16)
    probs = probs_ref[0]
    values = jnp.concatenate(
        [(probs[:, 0:1] * dmixed).astype(BF16), (probs[:, 1:2] * dmixed).astype(BF16)], axis=0
    )
    slots = out_refs[0].shape[0]
    spots = lax.broadcasted_iota(jnp.int32, (slots * group_count, 2 * rows), 0)
    hot = jnp.where(spots == flat_row_ref[0], 1.0, 0.0).astype(BF16)
    placed = jnp.dot(hot, values, preferred_element_type=F32).astype(BF16)
    for e in range(group_count):
        out_refs[e][...] = placed[e * slots : (e + 1) * slots]
    p0 = jnp.sum(dmixed * picked_ref[0].astype(F32), axis=1, keepdims=True)
    p1 = jnp.sum(dmixed * picked_ref[1].astype(F32), axis=1, keepdims=True)
    two = lax.broadcasted_iota(jnp.int32, (rows, 2), 1)
    grad_probs_ref[0] = jnp.where(two == 0, p0, p1)
    part = width // group_count
    for e in range(group_count):
        share = kacc[:, e * part : (e + 1) * part] * scale
        if last_terms is not None:
            share = share + last_terms[e]
        terms_ref[e] = share


def whole(shape):
    return pl.BlockSpec(shape, lambda *_: (0,) * len(shape))


def of_micro(micro, shape):
    return pl.BlockSpec((1,) + shape[1:], lambda *_: (micro,) + (0,) * (len(shape) - 1))


def combine(micro, place, tables, frames, grad_out, flat, probs, gain):
    group_count = len(tables)
    rows, width = frames.shape[1:]
    return pl.pallas_call(
        functools.partial(combine_kernel, group_count),
        grid_spec=pltpu.PrefetchScalarGridSpec(
            num_scalar_prefetch=1,
            grid=(1,),
            in_specs=[whole(t.shape) for t in tables]
            + [
                of_micro(micro, frames.shape),
                of_micro(micro, grad_out.shape),
                of_micro(micro, flat.shape),
                of_micro(micro, probs.shape),
                whole(gain.shape),
            ],
            out_specs=[
                whole((SIDE + GSIDE, width)),
                whole((SIDE + GSIDE, width)),
                whole((rows, width)),
                whole((rows, 128)),
                whole((2, rows, width)),
            ],
        ),
        out_shape=[
            jax.ShapeDtypeStruct((SIDE + GSIDE, width), BF16),
            jax.ShapeDtypeStruct((SIDE + GSIDE, width), BF16),
            jax.ShapeDtypeStruct((rows, width), F32),
            jax.ShapeDtypeStruct((rows, 128), F32),
            jax.ShapeDtypeStruct((2, rows, width), BF16),
        ],
        compiler_params=pltpu.CompilerParams(vmem_limit_bytes=VMEM_LIMIT),
        cost_estimate=pl.CostEstimate(flops=3000 * 10**6, bytes_accessed=0, transcendentals=0),
        name="combine",
    )(place, *tables, frames, grad_out, flat, probs, gain)


def conv(micro, place, lengths, group_count, frame_total, near, far, grad_out, nhat, rstd, picked, flat_row, probs, gain, kernel, earlier):
    rows, width = nhat.shape
    micro_count = grad_out.shape[0]
    first = earlier is None
    slots = EXPERTS * CAP // group_count
    mid = rows + 2 * GSIDE
    full = rows + 2 * SIDE
    terms_shape = (group_count, KW + 1, width // group_count)
    in_specs = [
        whole(near.shape),
        whole(far.shape),
        of_micro(micro, grad_out.shape),
        whole(nhat.shape),
        whole(rstd.shape),
        whole(picked.shape),
        of_micro(micro, flat_row.shape),
        of_micro(micro, probs.shape),
        whole(gain.shape),
        whole(kernel.shape),
    ]
    operands = [place, lengths, near, far, grad_out, nhat, rstd, picked, flat_row, probs, gain, kernel]
    aliases = {}
    if not first:
        in_specs += [whole(terms_shape), pl.BlockSpec(memory_space=pl.ANY), pl.BlockSpec(memory_space=pl.ANY)]
        aliases = {len(operands) + 1: 0, len(operands) + 2: 1}
        operands += [earlier[2], earlier[0], earlier[1]]
    return pl.pallas_call(
        functools.partial(
            conv_kernel, group_count, first, micro, frame_total, 1.0 / math.sqrt(micro_count * frame_total)
        ),
        grid_spec=pltpu.PrefetchScalarGridSpec(
            num_scalar_prefetch=2,
            grid=(1,),
            in_specs=in_specs,
            out_specs=[
                of_micro(micro, grad_out.shape),
                of_micro(micro, probs.shape),
                whole(terms_shape),
            ]
            + [whole((slots, width))] * group_count,
            scratch_shapes=[
                pltpu.VMEM((full, width), BF16),
                pltpu.VMEM((mid, width), BF16),
                pltpu.VMEM((KW * mid, full), BF16),
                pltpu.VMEM((full, width), BF16),
                pltpu.VMEM((KW + 1, width), F32),
            ],
        ),
        out_shape=[
            jax.ShapeDtypeStruct((micro_count, rows, width), BF16),
            jax.ShapeDtypeStruct(probs.shape, F32),
            jax.ShapeDtypeStruct(terms_shape, F32),
        ]
        + [jax.ShapeDtypeStruct((slots, width), BF16)] * group_count,
        input_output_aliases=aliases,
        compiler_params=pltpu.CompilerParams(vmem_limit_bytes=VMEM_LIMIT),
        cost_estimate=pl.CostEstimate(flops=8 * 10**9, bytes_accessed=0, transcendentals=0),
        name="conv",
    )(*operands)


def finish_kernel(group_count, micro, place_ref, *refs):
    blocks = refs[:group_count]
    out_ref, sems = refs[-2:]
    me = place_ref[2]
    copies = [
        pltpu.make_async_copy(block, out_ref.at[micro, jnp.bitwise_xor(me, step)], sems.at[step])
        for step, block in enumerate(blocks)
    ]
    for copy in copies:
        copy.start()
    for copy in copies:
        copy.wait()


def finish(micro, micro_count, place, blocks, earlier=None):
    group_count = len(blocks)
    slots, width = blocks[0].shape
    anywhere = pl.BlockSpec(memory_space=pl.ANY)
    operands = [place, *blocks]
    aliases = {}
    if earlier is not None:
        aliases = {len(operands): 0}
        operands.append(earlier)
    return pl.pallas_call(
        functools.partial(finish_kernel, group_count, micro),
        in_specs=[pl.BlockSpec(memory_space=pltpu.SMEM)] + [anywhere] * (len(operands) - 1),
        out_specs=anywhere,
        out_shape=jax.ShapeDtypeStruct((micro_count, group_count, slots, width), BF16),
        scratch_shapes=[pltpu.SemaphoreType.DMA((group_count,))],
        input_output_aliases=aliases,
        compiler_params=pltpu.CompilerParams(vmem_limit_bytes=SMALL_LIMIT),
        cost_estimate=pl.CostEstimate(flops=1500 * 10**6, bytes_accessed=0, transcendentals=0),
        name="finish",
    )(*operands)


def total_kernel(*refs):
    parts = refs[:-2]
    taps_ref, gain_ref = refs[-2:]
    total = parts[0][...]
    for part in parts[1:]:
        total = total + part[...]
    taps_ref[...] = total[:KW]
    gain_ref[...] = total[KW]


def total_of(parts):
    share = parts[0].shape[1]
    inside = pl.BlockSpec(memory_space=pltpu.VMEM)
    return pl.pallas_call(
        total_kernel,
        in_specs=[inside] * len(parts),
        out_specs=[inside, inside],
        out_shape=[jax.ShapeDtypeStruct((KW, share), F32), jax.ShapeDtypeStruct((share,), F32)],
        compiler_params=pltpu.CompilerParams(vmem_limit_bytes=SMALL_LIMIT),
        name="total",
    )(*parts)


def take(cells, index):
    return lax.dynamic_index_in_dim(cells, index, axis=0, keepdims=False)


def local(frames, expert_out, routes, order, probs, lengths, gain, kernel, grad_out):
    micro_count, rows, width = frames.shape
    groups = lax.axis_size("expert")
    tm = lax.axis_size("tm")
    both = ("tm", "expert")
    devices = groups * tm
    frame_total = rows * devices
    me = lax.axis_index("expert")
    here = lax.axis_index(both)
    odd = lax.rem(here, 2)
    place = jnp.stack([here * rows, odd, me]).astype(jnp.int32)
    per = EXPERTS // groups
    block = per * CAP
    near_pairs = [(i, i ^ 1) for i in range(devices)]
    far_pairs = [(i, (i - 1) % devices if i % 2 == 0 else (i + 1) % devices) for i in range(devices)]

    def swap(cells, step):
        return lax.ppermute(cells, "expert", [(i, i ^ step) for i in range(groups)])

    tables = []
    cells = expert_out
    sizes = (1, 1, 1) + expert_out.shape[3:]
    for micro in range(micro_count):
        blocks = [
            lax.dynamic_slice(cells, (micro, 0, me ^ step, 0, 0, 0), sizes).reshape(block, width)
            for step in range(groups)
        ]
        cells, *blocks = lax.optimization_barrier([cells, *blocks])
        tables.append([blocks[0]] + [swap(blocks[step], step) for step in range(1, groups)])

    slots = jax.vmap(slot_table)(routes, order[:, 0])
    flat = ((routes // per) ^ me) * block + (routes % per) * CAP + slots
    flat_row = jnp.swapaxes(flat, 1, 2).reshape(micro_count, 1, 2 * rows)
    gain_row = gain[None, :]

    earlier = None
    returned = []
    for micro in range(micro_count):
        near, far, nhat, rstd, picked = combine(
            micro, place, tables[micro], frames, grad_out, flat, probs, gain_row
        )
        near = lax.ppermute(near, both, near_pairs)
        far = lax.ppermute(far, both, far_pairs)
        grad_x, grad_probs, terms, *outs = conv(
            micro, place, lengths, groups, frame_total, near, far, grad_out,
            nhat, rstd, picked, flat_row, probs, gain_row, kernel, earlier,
        )
        earlier = (grad_x, grad_probs, terms)
        if returned:
            returned[-1][:2], terms = lax.optimization_barrier((returned[-1][:2], terms))
            returned[-1], outs = lax.optimization_barrier((returned[-1], outs))
        returned.append([outs[0]] + [swap(outs[step], step) for step in range(1, groups)])

    def over(cells, steps):
        return [lax.ppermute(cells, "tm", [(i, i ^ step) for i in range(tm)]) for step in steps]

    total = take(terms, me)
    for step in range(1, groups):
        total = total + swap(take(terms, me ^ step), step)
    step = 1
    while step < tm // 2:
        total = total + over(total, [step])[0]
        step *= 2
    parts = [total] + over(total, [step])
    grad_expert = None
    for micro in range(micro_count):
        grad_expert = finish(micro, micro_count, place, returned[micro], grad_expert)
    grad_kernel, grad_gain = total_of(parts)
    grad_expert = grad_expert.reshape(micro_count, 1, groups, per, CAP, width)
    return grad_x, grad_expert, grad_probs, grad_kernel, grad_gain


def solution(mesh):
    placed = (
        P(None, ("tm", "expert"), None),
        P(None, "tm", None, "expert", None, None),
        P(None, ("tm", "expert"), None),
        P(None, ("tm", "expert"), None),
        P(None, ("tm", "expert"), None),
        P(),
        P(),
        P(),
        P(None, ("tm", "expert"), None),
    )
    return jax.shard_map(
        local,
        mesh=mesh,
        in_specs=placed,
        out_specs=(
            P(None, ("tm", "expert"), None),
            P(None, "tm", None, "expert", None, None),
            P(None, ("tm", "expert"), None),
            P(None, "expert"),
            P("expert"),
        ),
        check_vma=False,
    )
```

```python
import functools
import math

import jax
import jax.numpy as jnp
from jax import lax
from jax.experimental import pallas as pl
from jax.experimental.pallas import tpu as pltpu
from jax.sharding import PartitionSpec as P

EXPERTS = 32
KW = 31
HALF = 15
CAP = 8
SIDE = 32
GSIDE = 16
F32 = jnp.float32
BF16 = jnp.bfloat16
VMEM_LIMIT = 12 * 1024 * 1024
SMALL_LIMIT = 4 * 1024 * 1024


def slot_table(route_rows, order_row):
    row_count = route_rows.shape[0]
    sort_keys = (order_row[:, None] * 2 + jnp.arange(2, dtype=jnp.int32)[None, :]).reshape(-1)
    owners = route_rows.reshape(-1)
    before = (owners[:, None] == owners[None, :]) & (sort_keys[None, :] < sort_keys[:, None])
    return jnp.sum(before.astype(jnp.int32), axis=1).reshape(row_count, 2)


def combine_kernel(
    group_count,
    place_ref,
    *rest,
):
    table_refs = rest[:group_count]
    frames_ref, grad_out_ref, flat_ref, probs_ref, gain_ref = rest[group_count : group_count + 5]
    near_ref, far_ref, nhat_ref, rstd_ref, picked_ref = rest[-5:]
    rows = frames_ref.shape[1]
    width = frames_ref.shape[2]
    flat = flat_ref[0]
    probs = probs_ref[0]
    table = jnp.concatenate([r[...] for r in table_refs], axis=0)
    lane = lax.broadcasted_iota(jnp.int32, (rows, table.shape[0]), 1)
    mixed = frames_ref[0].astype(F32)
    for k in range(2):
        hot = jnp.where(lane == flat[:, k : k + 1], 1.0, 0.0).astype(BF16)
        row = jnp.dot(hot, table, preferred_element_type=F32)
        picked_ref[k] = row.astype(BF16)
        mixed = mixed + probs[:, k : k + 1] * row
    mean = jnp.mean(mixed, axis=1, keepdims=True)
    centred = mixed - mean
    rstd = lax.rsqrt(jnp.mean(centred * centred, axis=1, keepdims=True) + 1e-05)
    nhat = centred * rstd
    nhat_ref[...] = nhat
    rstd_ref[...] = jnp.broadcast_to(rstd, rstd_ref.shape)
    conv_in = (nhat * gain_ref[...]).astype(BF16)
    odd = place_ref[1]

    def send(ref, first):
        ref[:SIDE] = conv_in[:SIDE] if first else conv_in[rows - SIDE :]
        ref[SIDE:] = grad_out_ref[0, :GSIDE] if first else grad_out_ref[0, rows - GSIDE :]

    @pl.when(odd == 0)
    def _():
        send(near_ref, False)
        send(far_ref, True)

    @pl.when(odd == 1)
    def _():
        send(near_ref, True)
        send(far_ref, False)


def swish_slope(values):
    sigmoid_v = jax.nn.sigmoid(values)
    return sigmoid_v * (1.0 + values * (1.0 - sigmoid_v))


def conv_kernel(
    group_count,
    first,
    micro,
    frame_total,
    scale,
    place_ref,
    lengths_ref,
    near_ref,
    far_ref,
    grad_out_ref,
    nhat_ref,
    rstd_ref,
    picked_ref,
    flat_row_ref,
    probs_ref,
    gain_ref,
    kernel_ref,
    *rest,
):
    if first:
        grad_x_ref, grad_probs_ref, terms_ref = rest[:3]
        rest = rest[3:]
        last_terms = None
    else:
        last_terms, _, _, grad_x_ref, grad_probs_ref, terms_ref = rest[:6]
        rest = rest[6:]
    out_refs = rest[:group_count]
    window, gout, shifts, gwin, kacc = rest[group_count:]
    rows, width = nhat_ref.shape
    conv_in = (nhat_ref[...] * gain_ref[...]).astype(BF16)
    mid = rows + 2 * GSIDE
    full = rows + 2 * SIDE
    odd = place_ref[1]

    window[SIDE : SIDE + rows, :] = conv_in
    gout[GSIDE : GSIDE + rows, :] = grad_out_ref[0]

    def receive(before, after):
        window[:SIDE, :] = before[:SIDE]
        window[SIDE + rows :, :] = after[:SIDE]
        gout[:GSIDE, :] = before[SIDE:]
        gout[GSIDE + rows :, :] = after[SIDE:]

    @pl.when(odd == 0)
    def _():
        receive(far_ref, near_ref)

    @pl.when(odd == 1)
    def _():
        receive(near_ref, far_ref)

    gwin[: SIDE - GSIDE, :] = jnp.zeros((SIDE - GSIDE, width), BF16)
    gwin[SIDE - GSIDE + mid :, :] = jnp.zeros((SIDE - GSIDE, width), BF16)

    first_frame = place_ref[0]
    t_local = lax.broadcasted_iota(jnp.int32, (mid, full), 0)
    r_local = lax.broadcasted_iota(jnp.int32, (mid, full), 1)
    t_pos = first_frame - GSIDE + t_local
    r_pos = first_frame - SIDE + r_local

    def count(u, carry):
        end, t_seg, r_seg = carry
        end = end + lengths_ref[micro, u]
        return (
            end,
            t_seg + jnp.where(t_pos >= end, 1, 0),
            r_seg + jnp.where(r_pos >= end, 1, 0),
        )

    zero = jnp.zeros((mid, full), jnp.int32)
    _, t_seg, r_seg = lax.fori_loop(0, lengths_ref.shape[1], count, (0, zero, zero))
    same = (t_seg == r_seg) & (t_pos >= 0) & (t_pos < frame_total) & (r_pos >= 0) & (r_pos < frame_total)
    gap = jnp.where(same, r_local - t_local - (SIDE - GSIDE - HALF), -1)
    for i in range(KW):
        shifts[i * mid : (i + 1) * mid, :] = jnp.where(gap == i, 1.0, 0.0).astype(BF16)

    taps = kernel_ref[...]
    xw = window[...]
    acc = jnp.zeros((mid, width), F32)
    for i in range(KW):
        v = jnp.dot(shifts[i * mid : (i + 1) * mid, :], xw, preferred_element_type=F32)
        acc = acc + taps[i : i + 1, :] * v
    g = (gout[...].astype(F32) * swish_slope(acc)).astype(BF16)
    gwin[SIDE - GSIDE : SIDE - GSIDE + mid, :] = g
    gw = gwin[...]
    x = conv_in.astype(F32)
    acc = jnp.zeros((rows, width), F32)
    for j in range(KW):
        base = j * mid + GSIDE
        v = jnp.dot(shifts[base : base + rows, :], gw, preferred_element_type=F32)
        i = KW - 1 - j
        acc = acc + taps[i : i + 1, :] * v
        kacc[i : i + 1, :] = jnp.sum(x * v, axis=0, keepdims=True)
    grad_in = acc.astype(BF16).astype(F32)
    nhat = nhat_ref[...]
    kacc[KW : KW + 1, :] = jnp.sum(grad_in * nhat, axis=0, keepdims=True)
    dn = grad_in * gain_ref[...]
    m1 = jnp.sum(dn, axis=1, keepdims=True) * (1.0 / width)
    m2 = jnp.sum(dn * nhat, axis=1, keepdims=True) * (1.0 / width)
    rstd = rstd_ref[:, :1]
    dmixed = grad_out_ref[0].astype(F32) + rstd * (dn - m1 - nhat * m2)
    grad_x_ref[0] = dmixed.astype(BF16)
    probs = probs_ref[0]
    values = jnp.concatenate(
        [(probs[:, 0:1] * dmixed).astype(BF16), (probs[:, 1:2] * dmixed).astype(BF16)], axis=0
    )
    slots = out_refs[0].shape[0]
    spots = lax.broadcasted_iota(jnp.int32, (slots * group_count, 2 * rows), 0)
    hot = jnp.where(spots == flat_row_ref[0], 1.0, 0.0).astype(BF16)
    placed = jnp.dot(hot, values, preferred_element_type=F32).astype(BF16)
    for e in range(group_count):
        out_refs[e][...] = placed[e * slots : (e + 1) * slots]
    p0 = jnp.sum(dmixed * picked_ref[0].astype(F32), axis=1, keepdims=True)
    p1 = jnp.sum(dmixed * picked_ref[1].astype(F32), axis=1, keepdims=True)
    two = lax.broadcasted_iota(jnp.int32, (rows, 2), 1)
    grad_probs_ref[0] = jnp.where(two == 0, p0, p1)
    part = width // group_count
    for e in range(group_count):
        share = kacc[:, e * part : (e + 1) * part] * scale
        if last_terms is not None:
            share = share + last_terms[e]
        terms_ref[e] = share


def whole(shape):
    return pl.BlockSpec(shape, lambda *_: (0,) * len(shape))


def of_micro(micro, shape):
    return pl.BlockSpec((1,) + shape[1:], lambda *_: (micro,) + (0,) * (len(shape) - 1))


def combine(micro, place, tables, frames, grad_out, flat, probs, gain):
    group_count = len(tables)
    rows, width = frames.shape[1:]
    return pl.pallas_call(
        functools.partial(combine_kernel, group_count),
        grid_spec=pltpu.PrefetchScalarGridSpec(
            num_scalar_prefetch=1,
            grid=(1,),
            in_specs=[whole(t.shape) for t in tables]
            + [
                of_micro(micro, frames.shape),
                of_micro(micro, grad_out.shape),
                of_micro(micro, flat.shape),
                of_micro(micro, probs.shape),
                whole(gain.shape),
            ],
            out_specs=[
                whole((SIDE + GSIDE, width)),
                whole((SIDE + GSIDE, width)),
                whole((rows, width)),
                whole((rows, 128)),
                whole((2, rows, width)),
            ],
        ),
        out_shape=[
            jax.ShapeDtypeStruct((SIDE + GSIDE, width), BF16),
            jax.ShapeDtypeStruct((SIDE + GSIDE, width), BF16),
            jax.ShapeDtypeStruct((rows, width), F32),
            jax.ShapeDtypeStruct((rows, 128), F32),
            jax.ShapeDtypeStruct((2, rows, width), BF16),
        ],
        compiler_params=pltpu.CompilerParams(vmem_limit_bytes=VMEM_LIMIT),
        cost_estimate=pl.CostEstimate(flops=3000 * 10**6, bytes_accessed=0, transcendentals=0),
        name="combine",
    )(place, *tables, frames, grad_out, flat, probs, gain)


def conv(micro, place, lengths, group_count, frame_total, near, far, grad_out, nhat, rstd, picked, flat_row, probs, gain, kernel, earlier):
    rows, width = nhat.shape
    micro_count = grad_out.shape[0]
    first = earlier is None
    slots = EXPERTS * CAP // group_count
    mid = rows + 2 * GSIDE
    full = rows + 2 * SIDE
    terms_shape = (group_count, KW + 1, width // group_count)
    in_specs = [
        whole(near.shape),
        whole(far.shape),
        of_micro(micro, grad_out.shape),
        whole(nhat.shape),
        whole(rstd.shape),
        whole(picked.shape),
        of_micro(micro, flat_row.shape),
        of_micro(micro, probs.shape),
        whole(gain.shape),
        whole(kernel.shape),
    ]
    operands = [place, lengths, near, far, grad_out, nhat, rstd, picked, flat_row, probs, gain, kernel]
    aliases = {}
    if not first:
        in_specs += [whole(terms_shape), pl.BlockSpec(memory_space=pl.ANY), pl.BlockSpec(memory_space=pl.ANY)]
        aliases = {len(operands) + 1: 0, len(operands) + 2: 1}
        operands += [earlier[2], earlier[0], earlier[1]]
    return pl.pallas_call(
        functools.partial(
            conv_kernel, group_count, first, micro, frame_total, 1.0 / math.sqrt(micro_count * frame_total)
        ),
        grid_spec=pltpu.PrefetchScalarGridSpec(
            num_scalar_prefetch=2,
            grid=(1,),
            in_specs=in_specs,
            out_specs=[
                of_micro(micro, grad_out.shape),
                of_micro(micro, probs.shape),
                whole(terms_shape),
            ]
            + [whole((slots, width))] * group_count,
            scratch_shapes=[
                pltpu.VMEM((full, width), BF16),
                pltpu.VMEM((mid, width), BF16),
                pltpu.VMEM((KW * mid, full), BF16),
                pltpu.VMEM((full, width), BF16),
                pltpu.VMEM((KW + 1, width), F32),
            ],
        ),
        out_shape=[
            jax.ShapeDtypeStruct((micro_count, rows, width), BF16),
            jax.ShapeDtypeStruct(probs.shape, F32),
            jax.ShapeDtypeStruct(terms_shape, F32),
        ]
        + [jax.ShapeDtypeStruct((slots, width), BF16)] * group_count,
        input_output_aliases=aliases,
        compiler_params=pltpu.CompilerParams(vmem_limit_bytes=VMEM_LIMIT),
        cost_estimate=pl.CostEstimate(flops=8 * 10**9, bytes_accessed=0, transcendentals=0),
        name="conv",
    )(*operands)


def finish_kernel(group_count, micro, place_ref, *refs):
    blocks = refs[:group_count]
    out_ref, sems = refs[-2:]
    me = place_ref[2]
    copies = [
        pltpu.make_async_copy(block, out_ref.at[micro, jnp.bitwise_xor(me, step)], sems.at[step])
        for step, block in enumerate(blocks)
    ]
    for copy in copies:
        copy.start()
    for copy in copies:
        copy.wait()


def finish(micro, micro_count, place, blocks, earlier=None):
    group_count = len(blocks)
    slots, width = blocks[0].shape
    anywhere = pl.BlockSpec(memory_space=pl.ANY)
    operands = [place, *blocks]
    aliases = {}
    if earlier is not None:
        aliases = {len(operands): 0}
        operands.append(earlier)
    return pl.pallas_call(
        functools.partial(finish_kernel, group_count, micro),
        in_specs=[pl.BlockSpec(memory_space=pltpu.SMEM)] + [anywhere] * (len(operands) - 1),
        out_specs=anywhere,
        out_shape=jax.ShapeDtypeStruct((micro_count, group_count, slots, width), BF16),
        scratch_shapes=[pltpu.SemaphoreType.DMA((group_count,))],
        input_output_aliases=aliases,
        compiler_params=pltpu.CompilerParams(vmem_limit_bytes=SMALL_LIMIT),
        cost_estimate=pl.CostEstimate(flops=1500 * 10**6, bytes_accessed=0, transcendentals=0),
        name="finish",
    )(*operands)


def total_kernel(*refs):
    parts = refs[:-2]
    taps_ref, gain_ref = refs[-2:]
    total = parts[0][...]
    for part in parts[1:]:
        total = total + part[...]
    taps_ref[...] = total[:KW]
    gain_ref[...] = total[KW]


def total_of(parts):
    share = parts[0].shape[1]
    inside = pl.BlockSpec(memory_space=pltpu.VMEM)
    return pl.pallas_call(
        total_kernel,
        in_specs=[inside] * len(parts),
        out_specs=[inside, inside],
        out_shape=[jax.ShapeDtypeStruct((KW, share), F32), jax.ShapeDtypeStruct((share,), F32)],
        compiler_params=pltpu.CompilerParams(vmem_limit_bytes=SMALL_LIMIT),
        name="total",
    )(*parts)


def take(cells, index):
    return lax.dynamic_index_in_dim(cells, index, axis=0, keepdims=False)


def local(frames, expert_out, routes, order, probs, lengths, gain, kernel, grad_out):
    micro_count, rows, width = frames.shape
    groups = lax.axis_size("expert")
    tm = lax.axis_size("tm")
    both = ("tm", "expert")
    devices = groups * tm
    frame_total = rows * devices
    me = lax.axis_index("expert")
    here = lax.axis_index(both)
    odd = lax.rem(here, 2)
    place = jnp.stack([here * rows, odd, me]).astype(jnp.int32)
    per = EXPERTS // groups
    block = per * CAP
    near_pairs = [(i, i ^ 1) for i in range(devices)]
    far_pairs = [(i, (i - 1) % devices if i % 2 == 0 else (i + 1) % devices) for i in range(devices)]

    def swap(cells, step):
        return lax.ppermute(cells, "expert", [(i, i ^ step) for i in range(groups)])

    tables = []
    cells = expert_out
    sizes = (1, 1, 1) + expert_out.shape[3:]
    def block_of(cells, micro, step):
        return lax.dynamic_slice(cells, (micro, 0, me ^ step, 0, 0, 0), sizes).reshape(block, width)

    for micro in range(micro_count):
        blocks = [block_of(cells, micro, step) for step in range(1, groups)]
        cells, *blocks = lax.optimization_barrier([cells, *blocks])
        tables.append([None] + [swap(blocks[step - 1], step) for step in range(1, groups)])
    for micro in range(micro_count):
        tables[micro][0] = block_of(cells, micro, 0)

    slots = jax.vmap(slot_table)(routes, order[:, 0])
    flat = ((routes // per) ^ me) * block + (routes % per) * CAP + slots
    flat_row = jnp.swapaxes(flat, 1, 2).reshape(micro_count, 1, 2 * rows)
    gain_row = gain[None, :]

    earlier = None
    returned = []
    for micro in range(micro_count):
        near, far, nhat, rstd, picked = combine(
            micro, place, tables[micro], frames, grad_out, flat, probs, gain_row
        )
        near = lax.ppermute(near, both, near_pairs)
        far = lax.ppermute(far, both, far_pairs)
        grad_x, grad_probs, terms, *outs = conv(
            micro, place, lengths, groups, frame_total, near, far, grad_out,
            nhat, rstd, picked, flat_row, probs, gain_row, kernel, earlier,
        )
        earlier = (grad_x, grad_probs, terms)
        if returned:
            returned[-1][:2], terms = lax.optimization_barrier((returned[-1][:2], terms))
            returned[-1], outs = lax.optimization_barrier((returned[-1], outs))
        returned.append([outs[0]] + [swap(outs[step], step) for step in range(1, groups)])

    def over(cells, steps):
        return [lax.ppermute(cells, "tm", [(i, i ^ step) for i in range(tm)]) for step in steps]

    total = take(terms, me)
    for step in range(1, groups):
        total = total + swap(take(terms, me ^ step), step)
    step = 1
    while step < tm // 2:
        total = total + over(total, [step])[0]
        step *= 2
    parts = [total] + over(total, [step])
    grad_expert = None
    for micro in range(micro_count):
        grad_expert = finish(micro, micro_count, place, returned[micro], grad_expert)
    grad_kernel, grad_gain = total_of(parts)
    grad_expert = grad_expert.reshape(micro_count, 1, groups, per, CAP, width)
    return grad_x, grad_expert, grad_probs, grad_kernel, grad_gain


def solution(mesh):
    placed = (
        P(None, ("tm", "expert"), None),
        P(None, "tm", None, "expert", None, None),
        P(None, ("tm", "expert"), None),
        P(None, ("tm", "expert"), None),
        P(None, ("tm", "expert"), None),
        P(),
        P(),
        P(),
        P(None, ("tm", "expert"), None),
    )
    return jax.shard_map(
        local,
        mesh=mesh,
        in_specs=placed,
        out_specs=(
            P(None, ("tm", "expert"), None),
            P(None, "tm", None, "expert", None, None),
            P(None, ("tm", "expert"), None),
            P(None, "expert"),
            P("expert"),
        ),
        check_vma=False,
    )
```
